32 devices in a mesh: row: 16 (over z, x, core), col: 2 (over y).
Axes of the slice: x: 2, y: 2, z: 4, core: 2. Of those that a mesh axis runs over, the one named last changes fastest.
Arguments:
- a_blocks: bfloat16 [16, 2, 16, 128, 128], P('row', 'col'), may hold values from -6 to 6
- a_rows: int32 [16, 2, 16], P('row', 'col'), may hold values from 0 to 3
- b_blocks: bfloat16 [16, 2, 32, 128, 128], P('row', 'col'), may hold values from -0.25 to 0.25
- b_cols: int32 [16, 2, 32], P('row', 'col'), may hold values from 0 to 7
- pair_list: int32 [16, 2, 4, 2, 256], P('row', 'col'), may hold values from 0 to 31, as said below
- pair_count: int32 [16, 2, 4], P('row', 'col'), may hold values from 1 to 256, as said below
- row_order: int32 [16, 4], P('row'), may hold values from 0 to 3, each once within a row
Outputs:
- product_matrix: bfloat16 [8192, 2048], P('row', 'col')
The draws below stay inside these ranges and needn't reach their ends.
Inputs may be any that keep to these rules, and one draw needn't show every extreme that they name: pair_list[..., 0, :] names a left slot below 16 and pair_list[..., 1, :] a right slot below 32; no list of one device and stop names the same pair twice. `pair_count`: in every stop some device's list is full.
All inputs are finite; a program needn't handle non-finite values.
Results may differ from the reference program's by a relative error of at most 0.001.
Values may be sent and summed in bfloat16 or wider, within the bound.
No kernel may reach another device: no remote copies, remote signals or barrier semaphores. Data moves between devices by JAX's collectives and lax.ppermute only.
A program may use at most 64 MiB of HBM per device.

```python
import jax
import jax.numpy as jnp
from jax import lax

BS = 128
CROWS = 4
CCOLS = 8
A_SLOTS = 16
B_SLOTS = 32
PAIRS = 256
STOPS = 4
N_ROW = 16
N_COL = 2


def draw_pair_list(key, part):
    keys = jax.random.split(key, N_ROW * N_COL * STOPS)

    def pick_pairs(one_key):
        first_key = jax.random.fold_in(one_key, 21)
        second_key = jax.random.fold_in(one_key, 22)
        others = jax.random.permutation(first_key, A_SLOTS * B_SLOTS - 2)[:PAIRS - 2] + 1
        ends = jnp.array([0, A_SLOTS * B_SLOTS - 1], dtype=jnp.int32)
        chosen = jnp.concatenate([ends, others.astype(jnp.int32)], axis=0)
        chosen = jax.random.permutation(second_key, chosen)
        return jnp.stack([chosen // B_SLOTS, chosen % B_SLOTS], axis=0)
    pair_table = jax.vmap(pick_pairs)(keys)
    return pair_table.reshape(N_ROW, N_COL, STOPS, 2, PAIRS).astype(jnp.int32)


def draw_pair_count(key, part):
    first_key = jax.random.fold_in(key, 11)
    second_key = jax.random.fold_in(key, 12)
    spread = jax.random.randint(first_key, (N_ROW, N_COL, STOPS), 0, PAIRS)
    counts = 1 + spread * spread // PAIRS
    busiest = jax.random.randint(second_key, (STOPS,), 0, N_ROW * N_COL)
    flat_index = jnp.arange(N_ROW * N_COL, dtype=jnp.int32).reshape(N_ROW, N_COL, 1)
    return jnp.where(flat_index == busiest[None, None, :], PAIRS, counts).astype(jnp.int32)


def place_ends(values, rng, least, top_value):
    shape = values.shape
    spot = [jax.random.randint(jax.random.fold_in(rng, axis), (), 0, shape[axis]) for axis in range(len(shape))]
    values = values.at[tuple(spot)].set(least)
    longest = shape.index(max(shape))
    spot[longest] = (spot[longest] + 1) % shape[longest]
    return values.at[tuple(spot)].set(top_value)


def levels(stream_key, shape, shards, smallest, high):
    gain, own = 1.0, jax.random.fold_in(stream_key, 6)
    for dim, shards_of in shards:
        heights = jnp.exp(jax.random.uniform(jax.random.fold_in(own, dim), (shards_of,), jnp.float32, smallest / len(shards), high / len(shards)))
        gain = gain * jnp.repeat(heights, shape[dim] // shards_of).reshape([-1 if axis == dim else 1 for axis in range(len(shape))])
    return gain


def noise(key, extent, scale, limit, cuts=(), kind=jnp.bfloat16):
    drawn = jax.random.normal(key, extent, jnp.float32) * scale
    if len(cuts) > 0:
        drawn = levels(key, extent, cuts, -0.22, 0.18) * drawn
    return jnp.clip(drawn, min=-limit, max=limit).astype(kind)


def setup_inputs(seed: int = 0) -> dict:
    streams_of = jax.random.split(jax.random.key(seed), 8)
    return {
        "a_blocks": noise(streams_of[0], (N_ROW, N_COL, A_SLOTS, BS, BS), 1.0, 6.0, ((0, 16), (1, 2))),
        "a_rows": place_ends(jax.random.randint(streams_of[1], (N_ROW, N_COL, A_SLOTS), 0, CROWS), jax.random.fold_in(streams_of[1], 1), 0, CROWS - 1).astype(jnp.int32),
        "b_blocks": noise(streams_of[2], (N_ROW, N_COL, B_SLOTS, BS, BS), (BS * 4) ** -0.5, 0.25, ((0, 16), (1, 2))),
        "b_cols": place_ends(jax.random.randint(streams_of[3], (N_ROW, N_COL, B_SLOTS), 0, CCOLS), jax.random.fold_in(streams_of[3], 1), 0, CCOLS - 1).astype(jnp.int32),
        "pair_list": draw_pair_list(jax.random.fold_in(streams_of[7], 71), 0),
        "pair_count": draw_pair_count(jax.random.fold_in(streams_of[7], 71), 0),
        "row_order": jax.vmap(lambda own: jax.random.permutation(own, CROWS))(jax.random.split(streams_of[6], N_ROW)).reshape((N_ROW, CROWS)).astype(jnp.int32),
    }


def reference(a_blocks, a_rows, b_blocks, b_cols, pair_list, pair_count, row_order):
    n_slots = CROWS * CCOLS

    def per_device(device):
        row_index = device // N_COL
        col_index = device % N_COL
        accum = jnp.zeros((n_slots, BS, BS), jnp.float32)
        for stop in range(STOPS):
            source_col = (col_index + row_index + stop) % N_COL
            source_row = (row_index + col_index + stop) % N_ROW
            left_set = a_blocks[row_index, source_col].astype(jnp.float32)
            left_ids = a_rows[row_index, source_col]
            right_set = b_blocks[source_row, col_index].astype(jnp.float32)
            right_ids = b_cols[source_row, col_index]
            pick = pair_list[row_index, col_index, stop]
            products = jnp.einsum("pij,pjk->pik", left_set[pick[0]], right_set[pick[1]])
            is_live = (jnp.arange(PAIRS, dtype=jnp.int32) < pair_count[row_index, col_index, stop]).astype(jnp.float32)
            target = row_order[row_index][left_ids[pick[0]]] * CCOLS + right_ids[pick[1]]
            accum = accum + jax.ops.segment_sum(products * is_live[:, None, None], target, n_slots)
        panel = accum.reshape(CROWS, CCOLS, BS, BS).transpose(0, 2, 1, 3).reshape(CROWS * BS, CCOLS * BS)
        return panel.astype(jnp.bfloat16)

    panels = lax.map(per_device, jnp.arange(N_ROW * N_COL, dtype=jnp.int32))
    panels = panels.reshape(N_ROW, N_COL, CROWS * BS, CCOLS * BS).transpose(0, 2, 1, 3)
    return panels.reshape(N_ROW * CROWS * BS, N_COL * CCOLS * BS)
```

```python
import functools

import jax
import jax.numpy as jnp
from jax import lax
from jax.experimental import pallas as pl
from jax.experimental.pallas import tpu as pltpu
from jax.sharding import PartitionSpec as P

CCOLS = 8
GROUP = 4
UNROLL = 2
SHIFT = 16


def product_tables(left_row, right_col, pair_list, pair_count, left_base, zero_slot, n_rows):
    n_stops, _, n_pairs = pair_list.shape
    n_left, n_right = left_row.shape[1], right_col.shape[1]
    n_targets = n_rows * CCOLS
    n_groups = n_pairs // GROUP + n_targets
    n_groups += -n_groups % UNROLL
    left, right = pair_list[:, 0], pair_list[:, 1]
    pair_range = jnp.arange(n_pairs, dtype=jnp.int32)
    row = jnp.sum(jnp.where(left[..., None] == jnp.arange(n_left), left_row[:, None, :], 0), axis=2)
    col = jnp.sum(jnp.where(right[..., None] == jnp.arange(n_right), right_col[:, None, :], 0), axis=2)
    live = pair_range[None, :] < pair_count[:, None]
    target = jnp.where(live, row * CCOLS + col, n_targets)
    earlier = pair_range[None, :, None] > pair_range[None, None, :]
    rank = jnp.sum((target[:, :, None] == target[:, None, :]) & earlier, axis=2, dtype=jnp.int32)
    targets = jnp.arange(n_targets, dtype=jnp.int32)
    size = jnp.sum(target[:, None, :] == targets[None, :, None], axis=2, dtype=jnp.int32)
    groups = (size + GROUP - 1) // GROUP
    before = targets[None, :, None] > targets[None, None, :]
    first = jnp.sum(jnp.where(before, groups[:, None, :], 0), axis=2)
    own_first = jnp.sum(
        jnp.where(target[:, :, None] > targets[None, None, :], groups[:, None, :], 0), axis=2
    )
    place = jnp.where(live, own_first * GROUP + rank, -1)
    empty = zero_slot << SHIFT
    packed = ((left + left_base[:, None]) << SHIFT) + right - empty
    places = jnp.arange(n_groups * GROUP, dtype=jnp.int32)
    members = empty + jnp.sum(
        jnp.where(place[:, None, :] == places[None, :, None], packed[:, None, :], 0), axis=2
    )
    slots = jnp.arange(n_groups, dtype=jnp.int32)
    inside = (first[:, None, :] <= slots[None, :, None]) & (
        slots[None, :, None] < (first + groups)[:, None, :]
    )
    group_target = jnp.sum(jnp.where(inside, targets[None, None, :], 0), axis=2)
    return members, group_target, jnp.sum(groups, axis=1)


def products_kernel(n_sets, opens, closes, n_groups, stop_ref, count_ref, member_ref, target_ref, left_ref, *refs):
    right_refs = refs[:n_sets]
    refs = refs[n_sets:]
    if not opens:
        start_ref, refs = refs[0], refs[1:]
    out_ref, refs = refs[0], refs[1:]
    total_ref = refs[0] if closes else out_ref
    edge = left_ref.shape[1]
    if opens:
        total_ref[...] = jnp.zeros_like(total_ref)
    else:
        total_ref[...] = start_ref[...]

    for which, right_ref in enumerate(right_refs):
        stop = stop_ref[which]

        def one_step(step, carry, right_ref=right_ref, stop=stop):
            for part in range(UNROLL):
                group = stop * n_groups + step * UNROLL + part
                codes = [member_ref[group * GROUP + member] for member in range(GROUP)]
                lefts = jnp.concatenate([left_ref[code >> SHIFT] for code in codes], axis=1)
                rights = jnp.concatenate(
                    [right_ref[code & ((1 << SHIFT) - 1)] for code in codes], axis=0
                )
                total_ref[target_ref[group]] += jnp.dot(
                    lefts, rights, preferred_element_type=jnp.float32
                )
            return carry

        lax.fori_loop(0, (count_ref[which] + UNROLL - 1) // UNROLL, one_step, 0)

    if closes:
        for target in range(total_ref.shape[0]):
            row, col = divmod(target, CCOLS)
            out_ref[row * edge : (row + 1) * edge, col * edge : (col + 1) * edge] = total_ref[
                target
            ].astype(out_ref.dtype)


def add_products(total, stops, tables, left_all, right_sets, n_rows, closes):
    members, group_target, group_count = tables
    n_stops, n_groups = group_target.shape
    edge = left_all.shape[1]
    n_targets = n_rows * CCOLS
    used = [(stop >= 0) & (stop < n_stops) for stop in stops]
    stops = [jnp.clip(stop, 0, n_stops - 1) for stop in stops]
    counts = jnp.stack([jnp.where(ok, group_count[stop], 0) for ok, stop in zip(used, stops)])
    vmem = pl.BlockSpec(memory_space=pltpu.VMEM)
    opens = total is None
    operands = [left_all, *right_sets] + ([] if opens else [total])
    if closes:
        out_shape = jax.ShapeDtypeStruct((n_rows * edge, CCOLS * edge), jnp.bfloat16)
        scratch = [pltpu.VMEM((n_targets, edge, edge), jnp.float32)]
    else:
        out_shape = jax.ShapeDtypeStruct((n_targets, edge, edge), jnp.float32)
        scratch = []
    return pl.pallas_call(
        functools.partial(products_kernel, len(right_sets), opens, closes, n_groups),
        out_shape=out_shape,
        grid_spec=pltpu.PrefetchScalarGridSpec(
            num_scalar_prefetch=4,
            in_specs=[vmem] * len(operands),
            out_specs=vmem,
            scratch_shapes=scratch,
        ),
        compiler_params=pltpu.CompilerParams(vmem_limit_bytes=40 << 20),
        cost_estimate=pl.CostEstimate(
            flops=2 * edge**3 * 1024, bytes_accessed=8 << 20, transcendentals=0
        ),
    )(jnp.stack(stops), counts, members.reshape(-1), group_target.reshape(-1), *operands)


def per_device(a_blocks, a_rows, b_blocks, b_cols, pair_list, pair_count, row_order):
    left_own, right_own = a_blocks[0, 0], b_blocks[0, 0]
    pair_list, pair_count, order = pair_list[0, 0], pair_count[0, 0], row_order[0]
    n_stops = pair_list.shape[0]
    n_left, n_right = left_own.shape[0], right_own.shape[0]
    n_rows = order.shape[0]
    n_row, n_col = lax.axis_size("row"), lax.axis_size("col")
    row, col = lax.axis_index("row"), lax.axis_index("col")
    core = row % 2

    def from_ahead(block, axis, distance):
        size = lax.axis_size(axis)
        return lax.ppermute(block, axis, [((i + distance) % size, i) for i in range(size)])

    def from_partner(block, cores):
        route = [(i ^ 1, i) for i in range(n_row) if i % 2 in cores]
        return lax.ppermute(block, "row", route)

    ids = jnp.concatenate([a_rows[0, 0], b_cols[0, 0]])
    all_ids = lax.all_gather(ids, ("row", "col"), axis=0)
    lefts = [left_own] + [from_ahead(left_own, "col", j) for j in range(1, n_col)]
    reach = (n_col + n_stops - 2 + 1) // 2
    rights = [right_own] + [from_ahead(right_own, "row", 2 * j) for j in range(1, reach + 1)]
    swapped = [
        from_partner(rights[j], (0,) if j == 0 else (1,) if j == reach else (0, 1))
        for j in range(reach + 1)
    ]

    left_ids, right_ids = [], []
    for stop in range(n_stops):
        source = row * n_col + (col + row + stop) % n_col
        left_ids.append(lax.dynamic_index_in_dim(all_ids, source, 0, False)[:n_left])
        source = (row + col + stop) % n_row * n_col + col
        right_ids.append(lax.dynamic_index_in_dim(all_ids, source, 0, False)[n_left:])
    left_ids, right_ids = jnp.stack(left_ids), jnp.stack(right_ids)
    match = left_ids[:, :, None] == jnp.arange(n_rows, dtype=jnp.int32)
    left_row = jnp.sum(jnp.where(match, order[None, None, :], 0), axis=2)
    left_base = (row + jnp.arange(n_stops, dtype=jnp.int32)) % n_col * n_left
    tables = product_tables(
        left_row, right_ids, pair_list, pair_count, left_base, n_col * n_left, n_rows
    )
    left_all = jnp.concatenate(lefts + [jnp.zeros_like(left_own[:1])])

    batches = [[(rights[0], -col), (swapped[0], jnp.where(core == 0, 1 - col, -1))]]
    for j in range(1, reach):
        batches.append([(rights[j], 2 * j - col)])
        batches.append([(swapped[j], 2 * j + 1 - 2 * core - col)])
    batches.append(
        [
            (rights[reach], 2 * reach - col),
            (swapped[reach], jnp.where(core == 1, 2 * reach - 1 - col, -1)),
        ]
    )
    total = None
    for index, batch in enumerate(batches):
        total = add_products(
            total,
            [stop.astype(jnp.int32) for _, stop in batch],
            tables,
            left_all,
            [blocks for blocks, _ in batch],
            n_rows,
            index == len(batches) - 1,
        )
    return total


def solution(mesh):
    placed = (
        P("row", "col", None, None, None),
        P("row", "col", None),
        P("row", "col", None, None, None),
        P("row", "col", None),
        P("row", "col", None, None, None),
        P("row", "col", None),
        P("row", None),
    )
    return jax.shard_map(
        per_device, mesh=mesh, in_specs=placed, out_specs=P("row", "col"), check_vma=False
    )
```

```python
import functools

import jax
import jax.numpy as jnp
from jax import lax
from jax.experimental import pallas as pl
from jax.experimental.pallas import tpu as pltpu
from jax.sharding import PartitionSpec as P

CCOLS = 8
GROUP = 2
UNROLL = 4
HEAD = 16
LEFT_SHIFT, RIGHT_SHIFT = 12, 3


def product_tables(left_row, pair_list, pair_count, left_base, zero_slot, n_right, n_rows):
    n_stops, _, n_pairs = pair_list.shape
    n_left = left_row.shape[1]
    n_keys = n_right * n_rows
    n_groups = (n_pairs + n_keys * (GROUP - 1)) // GROUP
    n_groups += UNROLL + -n_groups % UNROLL
    left, right = pair_list[:, 0], pair_list[:, 1]
    pair_range = jnp.arange(n_pairs, dtype=jnp.int32)
    row = jnp.sum(jnp.where(left[..., None] == jnp.arange(n_left), left_row[:, None, :], 0), axis=2)
    live = pair_range[None, :] < pair_count[:, None]
    key = jnp.where(live, right * n_rows + row, n_keys)
    earlier = pair_range[None, :, None] > pair_range[None, None, :]
    rank = jnp.sum((key[:, :, None] == key[:, None, :]) & earlier, axis=2, dtype=jnp.int32)
    keys = jnp.arange(n_keys, dtype=jnp.int32)
    size = jnp.sum(key[:, None, :] == keys[None, :, None], axis=2, dtype=jnp.int32)
    groups = (size + GROUP - 1) // GROUP
    before = keys[None, :, None] > keys[None, None, :]
    first = jnp.sum(jnp.where(before, groups[:, None, :], 0), axis=2)
    own_first = jnp.sum(
        jnp.where(key[:, :, None] > keys[None, None, :], groups[:, None, :], 0), axis=2
    )
    place = jnp.where(live, own_first * GROUP + rank, -1)
    moved = left + left_base[:, None] - zero_slot
    places = jnp.arange(n_groups * GROUP, dtype=jnp.int32)
    members = zero_slot + jnp.sum(
        jnp.where(place[:, None, :] == places[None, :, None], moved[:, None, :], 0), axis=2
    )
    slots = jnp.arange(n_groups, dtype=jnp.int32)
    inside = (first[:, None, :] <= slots[None, :, None]) & (
        slots[None, :, None] < (first + groups)[:, None, :]
    )
    group_key = jnp.sum(jnp.where(inside, keys[None, None, :], 0), axis=2)
    starts = first.reshape(n_stops, n_right, n_rows)[:, :, 0]
    ends = jnp.sum(groups, axis=1)
    starts = jnp.concatenate([starts, ends[:, None]], axis=1)
    return members, group_key, starts


def products_kernel(pieces, n_rows, n_groups, n_right, opens, closes, *refs):
    stop_ref, low_ref, high_ref, col_ref, member_ref, key_ref, left_ref = refs[:7]
    right_refs, refs = refs[7 : 7 + len(pieces)], refs[7 + len(pieces) :]
    if not opens:
        start_ref, refs = refs[0], refs[1:]
    out_ref, refs = refs[0], refs[1:]
    total_ref = refs[0] if closes else out_ref
    edge = left_ref.shape[1]
    if opens:
        total_ref[...] = jnp.zeros_like(total_ref)
    else:
        total_ref[...] = start_ref[...]

    for which, (head, first_slot, n_slots) in enumerate(pieces):
        right_ref = right_refs[which]
        base = stop_ref[which] * n_groups

        def block(ref, slot, head):
            return ref[pl.ds(pl.multiple_of(slot * edge + head, 16), edge), :]

        def one_step(step, carry):
            start = low_ref[which] + step * UNROLL
            for part in range(UNROLL):
                group = start + part
                inside = group < high_ref[which]
                key = key_ref[base + group]
                slot = key // n_rows
                target = (key % n_rows) * CCOLS + col_ref[which * n_right + slot]
                slot = jnp.clip(slot - first_slot, 0, n_slots - 1)
                lefts = []
                for member in range(GROUP):
                    left = member_ref[(base + group) * GROUP + member]
                    left = jnp.where(inside, left, left_ref.shape[0] // edge - 1)
                    lefts.append(block(left_ref, left, 0))
                right = block(right_ref, slot, head)
                total_ref[target] += jnp.dot(
                    jnp.concatenate(lefts, axis=1),
                    jnp.concatenate([right] * GROUP, axis=0),
                    preferred_element_type=jnp.float32,
                )
            return carry

        count = high_ref[which] - low_ref[which]
        lax.fori_loop(0, (count + UNROLL - 1) // UNROLL, one_step, 0)

    if closes:
        for target in range(total_ref.shape[0]):
            row, col = divmod(target, CCOLS)
            out_ref[row * edge : (row + 1) * edge, col * edge : (col + 1) * edge] = total_ref[
                target
            ].astype(out_ref.dtype)


def add_products(total, pieces, tables, left_all, n_right, n_rows, closes):
    members, group_key, starts = tables
    n_stops, n_groups = group_key.shape
    edge = left_all.shape[1]
    n_targets = n_rows * CCOLS
    stops, lows, highs, cols, layout = [], [], [], [], []
    for _, head, first_slot, n_slots, ids, stop in pieces:
        used = (stop >= 0) & (stop < n_stops)
        stop = jnp.clip(stop, 0, n_stops - 1).astype(jnp.int32)
        stops.append(stop)
        lows.append(starts[stop, first_slot])
        highs.append(jnp.where(used, starts[stop, first_slot + n_slots], lows[-1]))
        cols.append(ids)
        layout.append((head, first_slot, n_slots))
    vmem = pl.BlockSpec(memory_space=pltpu.VMEM)
    opens = total is None
    operands = [left_all] + [piece[0] for piece in pieces] + ([] if opens else [total])
    if closes:
        out_shape = jax.ShapeDtypeStruct((n_rows * edge, CCOLS * edge), jnp.bfloat16)
        scratch = [pltpu.VMEM((n_targets, edge, edge), jnp.float32)]
    else:
        out_shape = jax.ShapeDtypeStruct((n_targets, edge, edge), jnp.float32)
        scratch = []
    return pl.pallas_call(
        functools.partial(
            products_kernel, tuple(layout), n_rows, n_groups, n_right, opens, closes
        ),
        out_shape=out_shape,
        grid_spec=pltpu.PrefetchScalarGridSpec(
            num_scalar_prefetch=6,
            in_specs=[vmem] * len(operands),
            out_specs=vmem,
            scratch_shapes=scratch,
        ),
        compiler_params=pltpu.CompilerParams(vmem_limit_bytes=40 << 20),
        cost_estimate=pl.CostEstimate(flops=edge, bytes_accessed=edge, transcendentals=0),
    )(
        jnp.stack(stops),
        jnp.stack(lows),
        jnp.stack(highs),
        jnp.concatenate(cols),
        members.reshape(-1),
        group_key.reshape(-1),
        *operands,
    )


def per_device(a_blocks, a_rows, b_blocks, b_cols, pair_list, pair_count, row_order):
    pair_list, pair_count, order = pair_list[0, 0], pair_count[0, 0], row_order[0]
    n_stops = pair_list.shape[0]
    n_left, n_right, edge = a_blocks.shape[2], b_blocks.shape[2], a_blocks.shape[3]
    n_rows = order.shape[0]
    n_row, n_col = lax.axis_size("row"), lax.axis_size("col")
    row, col = lax.axis_index("row"), lax.axis_index("col")
    core, side = row % 2, row // 2 % 2
    reach = n_col + n_stops - 2
    half = n_right // 2

    def with_ids(blocks, ids):
        head = jnp.zeros((HEAD, edge), blocks.dtype)
        head = head.at[0, : ids.shape[0]].set(ids.astype(blocks.dtype))
        return jnp.concatenate([head, blocks.reshape(-1, edge)])

    def ids_of(blocks, count):
        return blocks[0, :count].astype(jnp.int32)

    def from_ahead(block, axis, distance):
        size = lax.axis_size(axis)
        return lax.ppermute(block, axis, [((i + distance) % size, i) for i in range(size)])

    def from_partner(block, bit, sides):
        route = [(i ^ bit, i) for i in range(n_row) if i // bit % 2 in sides]
        return lax.ppermute(block, "row", route)

    cut = HEAD + half * edge

    def halves(blocks):
        return blocks[:cut], blocks[cut:]

    right_own = b_blocks[0, 0].reshape(-1, edge)
    right_sent = with_ids(right_own, b_cols[0, 0])
    chips = (reach + 1) // 2
    far = [halves(right_sent)]
    for i in range(1, (chips + 1) // 2 + 1):
        far.append(tuple(from_ahead(part, "row", 4 * i) for part in far[0]))
    near = [halves(from_partner(right_sent, 2, (0,)))]
    left_sent = with_ids(a_blocks[0, 0], a_rows[0, 0])
    lefts = [left_sent] + [from_ahead(left_sent, "col", j) for j in range(1, n_col)]
    swap_own = from_partner(right_sent, 1, (0,))
    ahead, lefts = lax.optimization_barrier(([part[0] for part in far[1:]], lefts))

    def pass_on(i, part):
        sides = [s for s in (0, 1) if 2 * i + 1 - 2 * s <= chips]
        return from_partner(part, 2, sides)

    near += [[pass_on(i + 1, part)] for i, part in enumerate(ahead)]

    left_ids = jnp.stack([ids_of(left, n_left) for left in lefts])
    left_ahead = (row + jnp.arange(n_stops, dtype=jnp.int32)) % n_col
    match = left_ids[left_ahead][:, :, None] == jnp.arange(n_rows, dtype=jnp.int32)
    left_row = jnp.sum(jnp.where(match, order[None, None, :], 0), axis=2)
    tables = product_tables(
        left_row, pair_list, pair_count, left_ahead * n_left, n_col * n_left, n_right, n_rows
    )
    left_all = jnp.concatenate(
        [left[HEAD:] for left in lefts] + [jnp.zeros((edge, edge), left_sent.dtype)]
    )

    def add(total, pieces, closes=False):
        return add_products(total, pieces, tables, left_all, n_right, n_rows, closes)

    def cores_for(j):
        return [c for c in (0, 1) if 1 <= 2 * j + 1 - 2 * c <= reach]

    def swapped_stop(j):
        cores = cores_for(j)
        used = (core == 0) if cores == [0] else (core == 1) if cores == [1] else True
        return jnp.where(used, 2 * j + 1 - 2 * core - col, -1)

    total = add(
        None,
        [
            (right_own, 0, 0, n_right, b_cols[0, 0], -col),
            (swap_own, HEAD, 0, n_right, ids_of(swap_own, n_right), swapped_stop(0)),
        ],
    )

    def piece(blocks, part, ids, stop):
        return (blocks, 0 if part else HEAD, half if part else 0, half, ids, stop)

    ahead, behind, total = lax.optimization_barrier((ahead, [part[1] for part in far[1:]], total))
    for i, part in enumerate(behind):
        near[i + 1].append(pass_on(i + 1, part))
    for j in range(2, chips + 1, 2):
        arrived = ahead[j // 2 - 1], behind[j // 2 - 1]
        swapped = [from_partner(part, 1, cores_for(j)) for part in arrived]
        ids = ids_of(arrived[0], n_right), ids_of(swapped[0], n_right)
        pieces = []
        for part in range(2):
            pieces.append(piece(arrived[part], part, ids[0], 2 * j - col))
            pieces.append(piece(swapped[part], part, ids[1], swapped_stop(j)))
        total = add(total, pieces)

    odd_ids = {}
    for part in range(2):
        pieces = []
        if part == 1:
            late, total = lax.optimization_barrier(([sets[1] for sets in near], total))
            near = [(None, sets) for sets in late]
        for j in range(1, chips + 1, 2):
            arrived = jnp.where(side == 0, near[j // 2][part], near[j // 2 + 1][part])
            swapped = from_partner(arrived, 1, cores_for(j))
            if part == 0:
                odd_ids[j] = ids_of(arrived, n_right), ids_of(swapped, n_right)
            pieces.append(piece(arrived, part, odd_ids[j][0], 2 * j - col))
            pieces.append(piece(swapped, part, odd_ids[j][1], swapped_stop(j)))
        total = add(total, pieces, closes=part == 1)
    return total


def solution(mesh):
    placed = (
        P("row", "col", None, None, None),
        P("row", "col", None),
        P("row", "col", None, None, None),
        P("row", "col", None),
        P("row", "col", None, None, None),
        P("row", "col", None),
        P("row", None),
    )
    return jax.shard_map(
        per_device, mesh=mesh, in_specs=placed, out_specs=P("row", "col"), check_vma=False
    )
```

```python
import functools

import jax
import jax.numpy as jnp
from jax import lax
from jax.experimental import pallas as pl
from jax.experimental.pallas import tpu as pltpu
from jax.sharding import PartitionSpec as P

CCOLS = 8
UNROLL = 16
HEAD = 16
VMEM_BYTES = 40 << 20
VMEM = pl.BlockSpec(memory_space=pltpu.VMEM)


def round_up(value, step):
    return value + -value % step


class Sizes:
    def __init__(self, n_stops, n_pairs, n_left, n_right, n_rows, n_col, edge):
        self.n_stops, self.n_pairs, self.n_rows, self.n_col = n_stops, n_pairs, n_rows, n_col
        self.n_left, self.n_right, self.edge = n_left, n_right, edge
        self.half = n_right // 2
        self.zero_slot = n_col * n_left
        self.row_bits = (n_rows - 1).bit_length()
        self.key_bits = self.row_bits + (self.half - 1).bit_length()
        self.left_bits = self.zero_slot.bit_length()
        most = (n_pairs + self.half * n_rows) // 2
        self.width = round_up(round_up(most, UNROLL) + 1, 128)


def kernel_call(kernel, out_shape, operands, scalars=(), scratch=()):
    return pl.pallas_call(
        kernel,
        out_shape=out_shape,
        grid_spec=pltpu.PrefetchScalarGridSpec(
            num_scalar_prefetch=len(scalars),
            in_specs=[VMEM] * len(operands),
            out_specs=jax.tree.map(lambda _: VMEM, out_shape),
            scratch_shapes=list(scratch),
        ),
        compiler_params=pltpu.CompilerParams(vmem_limit_bytes=VMEM_BYTES),
        cost_estimate=pl.CostEstimate(flops=128, bytes_accessed=128, transcendentals=0),
    )(*scalars, *operands)


def pack_kernel(blocks_ref, ids_ref, *refs):
    part_refs, head_ref = refs[:-1], refs[-1]
    head_ref[...] = jnp.zeros_like(head_ref)
    head_ref[0:1, : ids_ref.shape[1]] = ids_ref[...].astype(jnp.float32)
    head = head_ref[...].astype(blocks_ref.dtype)
    rows = blocks_ref.shape[0] // len(part_refs)
    for part, ref in enumerate(part_refs):
        ref[:HEAD, :] = head
        ref[HEAD:, :] = blocks_ref[part * rows : (part + 1) * rows, :]


def pack(blocks, ids, parts):
    edge = blocks.shape[-1]
    blocks = blocks.reshape(-1, edge)
    shape = (HEAD + blocks.shape[0] // parts, edge)
    return kernel_call(
        pack_kernel,
        [jax.ShapeDtypeStruct(shape, blocks.dtype)] * parts,
        [blocks, ids.reshape(1, -1)],
        scratch=[pltpu.VMEM((HEAD, edge), jnp.float32)],
    )


def ids_of(ref):
    return ref[:HEAD, :].astype(jnp.float32)[0:1, :]


def prepare_kernel(sizes, count_ref, order_ref, pairs_ref, *refs):
    n_col, n_rows, half = sizes.n_col, sizes.n_rows, sizes.half
    left_refs, (words_ref, all_ref) = refs[:n_col], refs[n_col:]
    n_pairs, width = sizes.n_pairs, sizes.width
    rows = sizes.n_left * sizes.edge
    for j in range(n_col):
        all_ref[j * rows : (j + 1) * rows, :] = left_refs[j][HEAD:, :]
    all_ref[n_col * rows :, :] = jnp.zeros((sizes.edge, sizes.edge), all_ref.dtype)

    def total(mask, value, axis):
        return jnp.sum(jnp.where(mask, value, 0.0), axis=axis, keepdims=True)

    here = lax.axis_index("row")
    id_sets = [ids_of(ref) for ref in left_refs]
    lane = lax.broadcasted_iota(jnp.int32, (n_pairs, 128), 1)
    down = lax.broadcasted_iota(jnp.int32, (n_pairs, 1), 0)
    across = lax.broadcasted_iota(jnp.int32, (1, n_pairs), 1)
    places = lax.broadcasted_iota(jnp.int32, (1, width), 1).astype(jnp.float32)
    dead = float(sizes.n_right * n_rows)
    lefts, keys = [], []
    key_matrix = jnp.zeros((n_pairs, 128), jnp.float32)
    for stop in range(sizes.n_stops):
        ahead = lax.rem(here + stop, n_col)
        ids = id_sets[0]
        for j in range(1, n_col):
            ids = jnp.where(ahead == j, id_sets[j], ids)
        left_row = jnp.zeros_like(ids)
        for i in range(n_rows):
            left_row = jnp.where(ids == float(i), order_ref[i].astype(jnp.float32), left_row)
        left = pairs_ref[:, 2 * stop : 2 * stop + 1]
        right = pairs_ref[:, 2 * stop + 1 : 2 * stop + 2]
        row = total(lane == left, left_row, 1)
        key = right.astype(jnp.float32) * n_rows + row
        key = jnp.where(down < count_ref[stop], key, dead)
        lefts.append(((left + ahead * sizes.n_left) - sizes.zero_slot).astype(jnp.float32))
        keys.append(key)
        key_matrix = jnp.where(lane == stop, key, key_matrix)
    key_rows = key_matrix.T
    cut = float(half * n_rows)
    scale = [float(1 << sizes.key_bits), float(1 << (sizes.key_bits + sizes.left_bits))]
    empty = sizes.zero_slot * (scale[0] + scale[1])
    for stop in range(sizes.n_stops):
        left, key, other = lefts[stop], keys[stop], key_rows[stop : stop + 1, :]
        same = key == other
        rank = total(same & (across < down), 1.0, 1)
        other_rank = total(same & (down < across), 1.0, 0)
        other_opens = other_rank == 2.0 * jnp.floor(other_rank * 0.5)
        late, other_late = jnp.where(key >= cut, 1.0, 0.0), jnp.where(other >= cut, 1.0, 0.0)
        group = jnp.floor(rank * 0.5)
        opens = rank == 2.0 * group
        group += total((other < key) & (late == other_late) & other_opens, 1.0, 1)
        part = jnp.where(opens, left * scale[0] + key - late * cut, left * scale[1])
        for which in range(2):
            counted = (late == float(which)) & (key < dead)
            words = empty + total(counted & (group == places), part, 0)
            words = jnp.where(places == width - 1.0, total(counted & opens, 1.0, 0), words)
            words_ref[2 * stop + which : 2 * stop + which + 1, :] = words.astype(jnp.int32)


def products_kernel(sizes, layout, opens, closes, words_ref, left_ref, *refs):
    right_refs, refs = refs[: len(layout)], refs[len(layout) :]
    start_ref = None
    if not opens:
        start_ref, refs = refs[0], refs[1:]
    out_ref, ids_ref, col_ref, copy_sem = refs[:4]
    total_ref = refs[4] if closes else out_ref
    edge = sizes.edge
    for which, ref in enumerate(right_refs):
        ids_ref[which : which + 1, :] = ids_of(ref).astype(jnp.int32)
    copy = pltpu.make_async_copy(ids_ref, col_ref, copy_sem)
    copy.start()
    total_ref[...] = jnp.zeros_like(total_ref) if opens else start_ref[...]
    copy.wait()

    core, col = lax.rem(lax.axis_index("row"), 2), lax.axis_index("col")

    def block(ref, slot, head):
        return ref[pl.ds(pl.multiple_of(slot * edge + head, HEAD), edge), :]

    for which, (part, ahead) in enumerate(layout):
        right_ref = right_refs[which]
        stop = jnp.where(
            core == 0,
            -1 if ahead[0] is None else ahead[0] - col,
            -1 if ahead[1] is None else ahead[1] - col,
        )
        used = (stop >= 0) & (stop < sizes.n_stops)
        line = jnp.clip(stop, 0, sizes.n_stops - 1) * 2 + part
        count = jnp.where(used, words_ref[line, sizes.width - 1], 0)

        def one_step(step, carry, which=which, right_ref=right_ref, line=line):
            for member in range(UNROLL):
                word = words_ref[line, step * UNROLL + member]
                row = word & ((1 << sizes.row_bits) - 1)
                slot = (word & ((1 << sizes.key_bits) - 1)) >> sizes.row_bits
                word = word >> sizes.key_bits
                first = word & ((1 << sizes.left_bits) - 1)
                second = word >> sizes.left_bits
                target = row * CCOLS + col_ref[which, slot + part * sizes.half]
                right = block(right_ref, slot, HEAD)
                total_ref[target] += jnp.dot(
                    jnp.concatenate([block(left_ref, first, 0), block(left_ref, second, 0)], axis=1),
                    jnp.concatenate([right, right], axis=0),
                    preferred_element_type=jnp.float32,
                )
            return carry

        lax.fori_loop(0, (count + UNROLL - 1) // UNROLL, one_step, 0)

    if closes:
        for target in range(total_ref.shape[0]):
            row, col = divmod(target, CCOLS)
            out_ref[row * edge : (row + 1) * edge, col * edge : (col + 1) * edge] = total_ref[
                target
            ].astype(out_ref.dtype)


def per_device(a_blocks, a_rows, b_blocks, b_cols, pair_list, pair_count, row_order):
    n_row, n_col = lax.axis_size("row"), lax.axis_size("col")
    n_stops, n_pairs = pair_list.shape[2], pair_list.shape[4]
    sizes = Sizes(
        n_stops,
        n_pairs,
        a_blocks.shape[2],
        b_blocks.shape[2],
        row_order.shape[1],
        n_col,
        a_blocks.shape[3],
    )
    row = lax.axis_index("row")
    core, side = row % 2, row // 2 % 2
    reach = n_col + n_stops - 2
    chips = (reach + 1) // 2
    parts = range(2)

    def from_ahead(block, axis, distance):
        size = lax.axis_size(axis)
        return lax.ppermute(block, axis, [((i + distance) % size, i) for i in range(size)])

    def swap(bit, lower, upper):
        mine = jnp.where(row // bit % 2 == 1, upper, lower)
        return lax.ppermute(mine, "row", [(i ^ bit, i) for i in range(n_row)])

    own = pack(b_blocks, b_cols, 2)
    left_own = pack(a_blocks, a_rows, 1)[0]
    sets = {0: list(own)}
    for j in range(2, chips + 2, 2):
        sets[j] = [from_ahead(own[0], "row", 2 * j)]
    lefts = [left_own] + [from_ahead(left_own, "col", j) for j in range(1, n_col)]
    for j in range(2, chips + 2, 2):
        sets[j].append(from_ahead(own[1], "row", 2 * j))

    early = {j: sets[j][0] for j in sets}
    early, lefts = lax.optimization_barrier((early, lefts))
    odd = {j: [swap(2, early[j + 1], early[j - 1])] for j in range(1, chips + 1, 2)}
    pairs = pair_list.reshape(2 * n_stops, n_pairs).T
    words, left_all = kernel_call(
        functools.partial(prepare_kernel, sizes),
        [
            jax.ShapeDtypeStruct((2 * n_stops, sizes.width), jnp.int32),
            jax.ShapeDtypeStruct(((sizes.zero_slot + 1) * sizes.edge, sizes.edge), jnp.bfloat16),
        ],
        [pairs] + lefts,
        [pair_count.reshape(-1), row_order.reshape(-1)],
    )

    def add(total, pieces, closes=False):
        edge, n_targets = sizes.edge, sizes.n_rows * CCOLS
        layout = tuple((part, ahead) for _, part, ahead in pieces)
        sums = (n_targets, edge, edge)
        if closes:
            out_shape = jax.ShapeDtypeStruct((sizes.n_rows * edge, CCOLS * edge), jnp.bfloat16)
        else:
            out_shape = jax.ShapeDtypeStruct(sums, jnp.float32)
        lines = round_up(len(pieces), 8)
        return kernel_call(
            functools.partial(products_kernel, sizes, layout, total is None, closes),
            out_shape,
            [left_all] + [blocks for blocks, _, _ in pieces] + ([] if total is None else [total]),
            [words],
            [
                pltpu.VMEM((lines, 128), jnp.int32),
                pltpu.SMEM((lines, 128), jnp.int32),
                pltpu.SemaphoreType.DMA,
            ]
            + ([pltpu.VMEM(sums, jnp.float32)] if closes else []),
        )

    def both(distance):
        return (distance, distance)

    def swapped(j):
        ahead = 2 * j + 1, 2 * j - 1
        return tuple(d if 1 <= d <= reach else None for d in ahead)

    ends = (swapped(0)[0], swapped(chips)[1])
    evens = range(2, chips + 1, 2)
    odds = range(1, chips + 1, 2)

    total = add(None, [(own[part], part, both(0)) for part in parts])
    late = {j: sets[j][1] for j in sets if j}
    first_odd = [odd[j][0] for j in odds]
    early, late, first_odd, total = lax.optimization_barrier((early, late, first_odd, total))
    odd = {j: [arrived] for j, arrived in zip(odds, first_odd)}
    even_sets = {0: own, **{j: [early[j], late[j]] for j in late}}
    for j in odds:
        odd[j].append(swap(2, even_sets[j + 1][1], even_sets[j - 1][1]))
    pieces = []
    for part in parts:
        for j in evens:
            pieces.append((even_sets[j][part], part, both(2 * j)))
            if j < chips:
                mine = even_sets[j][part]
                pieces.append((swap(1, mine, mine), part, swapped(j)))
        if chips % 2 == 0:
            ended = swap(1, even_sets[chips][part], own[part])
            pieces.append((ended, part, ends))
    total = add(total, pieces)
    for part in parts:
        if part:
            late_odd, total = lax.optimization_barrier(([odd[j][1] for j in odds], total))
            for j, arrived in zip(odds, late_odd):
                odd[j][1] = arrived
        pieces = []
        for j in odds:
            pieces.append((odd[j][part], part, both(2 * j)))
            if j < chips:
                pieces.append((swap(1, odd[j][part], odd[j][part]), part, swapped(j)))
        if chips % 2:
            pieces.append((swap(1, odd[chips][part], own[part]), part, ends))
        total = add(total, pieces, closes=part == 1)
    return total


def solution(mesh):
    placed = (
        P("row", "col", None, None, None),
        P("row", "col", None),
        P("row", "col", None, None, None),
        P("row", "col", None),
        P("row", "col", None, None, None),
        P("row", "col", None),
        P("row", None),
    )
    return jax.shard_map(
        per_device, mesh=mesh, in_specs=placed, out_specs=P("row", "col"), check_vma=False
    )
```

```python
import functools

import jax
import jax.numpy as jnp
from jax import lax
from jax.experimental import pallas as pl
from jax.experimental.pallas import tpu as pltpu
from jax.sharding import PartitionSpec as P

CCOLS = 8
PARTS = 4
UNROLL = 16
HEAD = 16
VMEM_BYTES = 40 << 20
VMEM = pl.BlockSpec(memory_space=pltpu.VMEM)


def round_up(value, step):
    return value + -value % step


class Sizes:
    def __init__(self, n_stops, n_pairs, n_left, n_right, n_rows, n_col, edge):
        self.n_stops, self.n_pairs, self.n_rows, self.n_col = n_stops, n_pairs, n_rows, n_col
        self.n_left, self.n_right, self.edge = n_left, n_right, edge
        self.parts = PARTS
        self.per_part = n_right // PARTS
        self.zero_slot = n_col * n_left
        self.row_bits = (n_rows - 1).bit_length()
        self.key_bits = self.row_bits + (self.per_part - 1).bit_length()
        self.left_bits = self.zero_slot.bit_length()
        most = (n_pairs + self.per_part * n_rows) // 2
        self.width = round_up(round_up(most, UNROLL) + 1, 128)


def kernel_call(kernel, out_shape, operands, scalars=(), scratch=(), specs=None):
    return pl.pallas_call(
        kernel,
        out_shape=out_shape,
        grid_spec=pltpu.PrefetchScalarGridSpec(
            num_scalar_prefetch=len(scalars),
            in_specs=specs or [VMEM] * len(operands),
            out_specs=jax.tree.map(lambda _: VMEM, out_shape),
            scratch_shapes=list(scratch),
        ),
        compiler_params=pltpu.CompilerParams(vmem_limit_bytes=VMEM_BYTES),
        cost_estimate=pl.CostEstimate(flops=128, bytes_accessed=128, transcendentals=0),
    )(*scalars, *operands)


def pack_kernel(blocks_ref, ids_ref, *refs):
    part_refs, head_ref, sems = refs[:-2], refs[-2], refs[-1]
    rows = blocks_ref.shape[0] // len(part_refs)
    copies = [
        pltpu.make_async_copy(
            blocks_ref.at[pl.ds(part * rows, rows)], ref.at[pl.ds(HEAD, rows)], sems.at[part]
        )
        for part, ref in enumerate(part_refs)
    ]
    for copy in copies:
        copy.start()
    head_ref[...] = jnp.zeros_like(head_ref)
    head_ref[0:1, : ids_ref.shape[1]] = ids_ref[...].astype(jnp.float32)
    for ref in part_refs:
        ref[:HEAD, :] = head_ref[...].astype(ref.dtype)
    for copy in copies:
        copy.wait()


def pack(blocks, ids):
    edge = blocks.shape[-1]
    blocks = blocks.reshape(-1, edge)
    shape = (HEAD + blocks.shape[0] // PARTS, edge)
    return kernel_call(
        pack_kernel,
        [jax.ShapeDtypeStruct(shape, blocks.dtype)] * PARTS,
        [blocks, ids.reshape(1, -1)],
        scratch=[pltpu.VMEM((HEAD, edge), jnp.float32), pltpu.SemaphoreType.DMA((PARTS,))],
        specs=[pl.BlockSpec(memory_space=pl.ANY), VMEM],
    )


def choose_kernel(*refs):
    parts = (len(refs) - 2) // 2
    out_ref, sems = refs[-2], refs[-1]
    rows = refs[0].shape[0]
    core = lax.rem(lax.axis_index("row"), 2)
    for which in range(2):

        @pl.when(core == which)
        def _(which=which):
            copies = [
                pltpu.make_async_copy(
                    refs[which * parts + part], out_ref.at[pl.ds(part * rows, rows)], sems.at[part]
                )
                for part in range(parts)
            ]
            for copy in copies:
                copy.start()
            for copy in copies:
                copy.wait()


def choose(lower, upper):
    rows, edge = lower[0].shape
    return kernel_call(
        choose_kernel,
        jax.ShapeDtypeStruct((len(lower) * rows, edge), lower[0].dtype),
        [*lower, *upper],
        scratch=[pltpu.SemaphoreType.DMA((len(lower),))],
        specs=[pl.BlockSpec(memory_space=pl.ANY)] * (2 * len(lower)),
    )


def ids_of(ref):
    return ref[:HEAD, :].astype(jnp.float32)[0:1, :]


def prepare_kernel(sizes, count_ref, order_ref, pairs_ref, ids_ref, words_ref):
    n_col, n_rows, parts = sizes.n_col, sizes.n_rows, sizes.parts
    n_pairs, width = sizes.n_pairs, sizes.width

    def total(mask, value, axis):
        return jnp.sum(jnp.where(mask, value, 0.0), axis=axis, keepdims=True)

    here = lax.axis_index("row")
    lane = lax.broadcasted_iota(jnp.int32, (n_pairs, 128), 1)
    slot = lax.broadcasted_iota(jnp.int32, (n_pairs, sizes.n_left), 1)
    down = lax.broadcasted_iota(jnp.int32, (n_pairs, 1), 0)
    across = lax.broadcasted_iota(jnp.int32, (1, n_pairs), 1)
    places = lax.broadcasted_iota(jnp.int32, (1, width), 1).astype(jnp.float32)
    dead = float(sizes.n_right * n_rows)
    lefts, keys = [], []
    key_matrix = jnp.zeros((n_pairs, 128), jnp.float32)
    for stop in range(sizes.n_stops):
        ahead = lax.rem(here + stop, n_col)
        ids = ids_ref[0:1, :]
        for j in range(1, n_col):
            ids = jnp.where(ahead == j, ids_ref[j : j + 1, :], ids)
        left_row = jnp.zeros(ids.shape, jnp.float32)
        for i in range(n_rows):
            left_row = jnp.where(ids == i, order_ref[i].astype(jnp.float32), left_row)
        left = pairs_ref[:, 2 * stop : 2 * stop + 1]
        right = pairs_ref[:, 2 * stop + 1 : 2 * stop + 2]
        key = right.astype(jnp.float32) * n_rows + total(slot == left, left_row, 1)
        key = jnp.where(down < count_ref[stop], key, dead)
        lefts.append((left + ahead * sizes.n_left - sizes.zero_slot).astype(jnp.float32))
        keys.append(key)
        key_matrix = jnp.where(lane == stop, key, key_matrix)
    key_rows = key_matrix.T
    cut = float(sizes.per_part * n_rows)

    def part_of(key):
        return sum(jnp.where(key >= part * cut, 1.0, 0.0) for part in range(1, parts))

    scale = [float(1 << sizes.key_bits), float(1 << (sizes.key_bits + sizes.left_bits))]
    empty = sizes.zero_slot * (scale[0] + scale[1])
    for stop in range(sizes.n_stops):
        left, key, other = lefts[stop], keys[stop], key_rows[stop : stop + 1, :]
        same = key == other
        rank = total(same & (across < down), 1.0, 1)
        other_rank = total(same & (down < across), 1.0, 0)
        other_opens = other_rank == 2.0 * jnp.floor(other_rank * 0.5)
        own_part, other_part = part_of(key), part_of(other)
        group = jnp.floor(rank * 0.5)
        opens = rank == 2.0 * group
        group += total((other < key) & (own_part == other_part) & other_opens, 1.0, 1)
        word = jnp.where(opens, left * scale[0] + key - own_part * cut, left * scale[1])
        for part in range(parts):
            counted = (own_part == float(part)) & (key < dead)
            words = empty + total(counted & (group == places), word, 0)
            words = jnp.where(places == width - 1.0, total(counted & opens, 1.0, 0), words)
            line = parts * stop + part
            words_ref[line : line + 1, :] = words.astype(jnp.int32)


def products_kernel(sizes, n_rights, layout, opens, closes, words_ref, *refs):
    n_sources = sizes.n_col if opens else 1
    sources, refs = refs[:n_sources], refs[n_sources:]
    right_refs, refs = refs[:n_rights], refs[n_rights:]
    start_ref = None
    if not opens:
        start_ref, refs = refs[0], refs[1:]
    out_ref, refs = refs[0], refs[1:]
    left_ref = sources[0]
    edge = sizes.edge
    if opens:
        left_ref, refs = refs[0], refs[1:]
        rows = sizes.n_left * edge
        for j, source in enumerate(sources):
            left_ref[j * rows : (j + 1) * rows, :] = source[...]
        left_ref[len(sources) * rows :, :] = jnp.zeros((edge, edge), left_ref.dtype)
    ids_ref, col_ref, copy_sem = refs[:3]
    total_ref = refs[3] if closes else out_ref
    for which, ref in enumerate(right_refs):
        ids_ref[which : which + 1, :] = ids_of(ref).astype(jnp.int32)
    copy = pltpu.make_async_copy(ids_ref, col_ref, copy_sem)
    copy.start()
    total_ref[...] = jnp.zeros_like(total_ref) if opens else start_ref[...]
    copy.wait()

    core, col = lax.rem(lax.axis_index("row"), 2), lax.axis_index("col")

    def block(ref, slot, head):
        return ref[pl.ds(pl.multiple_of(slot * edge + head, HEAD), edge), :]

    for array, head, part, ahead in layout:
        stop = jnp.where(
            core == 0,
            -1 if ahead[0] is None else ahead[0] - col,
            -1 if ahead[1] is None else ahead[1] - col,
        )
        used = (stop >= 0) & (stop < sizes.n_stops)
        line = jnp.clip(stop, 0, sizes.n_stops - 1) * sizes.parts + part
        count = jnp.where(used, words_ref[line, sizes.width - 1], 0)

        def one_step(step, carry, array=array, head=head, part=part, line=line):
            for member in range(UNROLL):
                word = words_ref[line, step * UNROLL + member]
                row = word & ((1 << sizes.row_bits) - 1)
                slot = (word & ((1 << sizes.key_bits) - 1)) >> sizes.row_bits
                word = word >> sizes.key_bits
                first = word & ((1 << sizes.left_bits) - 1)
                second = word >> sizes.left_bits
                target = row * CCOLS + col_ref[array, slot + part * sizes.per_part]
                right = block(right_refs[array], slot, head + HEAD)
                total_ref[target] += jnp.dot(
                    jnp.concatenate([block(left_ref, first, 0), block(left_ref, second, 0)], axis=1),
                    jnp.concatenate([right, right], axis=0),
                    preferred_element_type=jnp.float32,
                )
            return carry

        lax.fori_loop(0, (count + UNROLL - 1) // UNROLL, one_step, 0)

    if closes:
        for target in range(total_ref.shape[0]):
            row, col = divmod(target, CCOLS)
            out_ref[row * edge : (row + 1) * edge, col * edge : (col + 1) * edge] = total_ref[
                target
            ].astype(out_ref.dtype)


def per_device(a_blocks, a_rows, b_blocks, b_cols, pair_list, pair_count, row_order):
    n_row, n_col = lax.axis_size("row"), lax.axis_size("col")
    n_stops, n_pairs = pair_list.shape[2], pair_list.shape[4]
    sizes = Sizes(
        n_stops,
        n_pairs,
        a_blocks.shape[2],
        b_blocks.shape[2],
        row_order.shape[1],
        n_col,
        a_blocks.shape[3],
    )
    row = lax.axis_index("row")
    edge, sums = sizes.edge, (sizes.n_rows * CCOLS, sizes.edge, sizes.edge)
    reach = n_col + n_stops - 2
    chips = (reach + 1) // 2
    evens, odds = range(2, chips + 1, 2), range(1, chips + 1, 2)
    parts = range(PARTS)

    def from_ahead(block, axis, distance):
        size = lax.axis_size(axis)
        return lax.ppermute(block, axis, [((i + distance) % size, i) for i in range(size)])

    def swap(bit, lower, upper):
        mine = lower if lower is upper else jnp.where(row // bit % 2 == 1, upper, lower)
        return lax.ppermute(mine, "row", [(i ^ bit, i) for i in range(n_row)])

    def both(distance):
        return (distance, distance)

    def swapped(j):
        ahead = 2 * j + 1, 2 * j - 1
        return tuple(d if 1 <= d <= reach else None for d in ahead)

    left_ids = [a_rows.reshape(1, -1)]
    left_ids += [from_ahead(left_ids[0], "col", j) for j in range(1, n_col)]
    own = list(pack(b_blocks, b_cols))
    even = {j: [from_ahead(part, "row", 2 * j) for part in own] for j in range(2, chips + 2, 2)}
    left_own = a_blocks.reshape(-1, edge)
    lefts = [left_own] + [from_ahead(left_own, "col", j) for j in range(1, n_col)]
    words = kernel_call(
        functools.partial(prepare_kernel, sizes),
        jax.ShapeDtypeStruct((PARTS * n_stops, sizes.width), jnp.int32),
        [pair_list.reshape(2 * n_stops, n_pairs).T, jnp.concatenate(left_ids)],
        [pair_count.reshape(-1), row_order.reshape(-1)],
    )

    def wait(part, *others):
        arrived, others = lax.optimization_barrier(([even[j][part] for j in even], others))
        for j, block in zip(even, arrived):
            even[j][part] = block
        return others

    def pass_on(part):
        sets = {0: own, **even}
        return {j: swap(2, sets[j + 1][part], sets[j - 1][part]) for j in odds}

    def add(total, pieces, closes=False):
        rights = list({id(piece[0]): piece[0] for piece in pieces}.values())
        places = {id(block): place for place, block in enumerate(rights)}
        layout = tuple((places[id(piece[0])], *piece[1:]) for piece in pieces)
        if closes:
            out_shape = jax.ShapeDtypeStruct((sizes.n_rows * edge, CCOLS * edge), jnp.bfloat16)
        else:
            out_shape = jax.ShapeDtypeStruct(sums, jnp.float32)
        if total is None:
            left_shape = ((sizes.zero_slot + 1) * edge, edge)
            out_shape = [out_shape, jax.ShapeDtypeStruct(left_shape, left_own.dtype)]
        lines = round_up(len(rights), 8)
        return kernel_call(
            functools.partial(
                products_kernel, sizes, len(rights), layout, total is None, closes
            ),
            out_shape,
            (lefts if total is None else [left_all])
            + rights
            + ([] if total is None else [total]),
            [words],
            [
                pltpu.VMEM((lines, 128), jnp.int32),
                pltpu.SMEM((lines, 128), jnp.int32),
                pltpu.SemaphoreType.DMA,
            ]
            + ([pltpu.VMEM(sums, jnp.float32)] if closes else []),
        )

    def pieces_of(j, part, block):
        pieces = [(block, 0, part, both(2 * j))]
        if j < chips:
            pieces.append((swap(1, block, block), 0, part, swapped(j)))
        return pieces

    def odd_pieces(part, sets):
        return [piece for j in odds for piece in pieces_of(j, part, sets[j])]

    def ends(sets):
        chosen = choose(sets, own)
        arrived = swap(1, chosen, chosen)
        ahead = swapped(0)[0], swapped(chips)[1]
        rows = own[0].shape[0]
        return [(arrived, part * rows, part, ahead) for part in parts]

    odd = {}
    (words,) = wait(0, words)
    odd[0] = pass_on(0)
    (lefts,) = wait(1, lefts)
    odd[1] = pass_on(1)
    total, left_all = add(None, [(own[part], 0, part, both(0)) for part in parts])
    odd[0], odd[1], total = wait(2, odd[0], odd[1], total)
    odd[2] = pass_on(2)
    pieces = odd_pieces(0, odd[0]) + odd_pieces(1, odd[1])
    total = add(total, pieces)
    odd[2], total = wait(3, odd[2], total)
    odd[3] = pass_on(3)
    pieces = [piece for j in evens for part in parts for piece in pieces_of(j, part, even[j][part])]
    if chips % 2 == 0:
        pieces += ends(even[chips])
    total = add(total, pieces)
    odd[3], total = lax.optimization_barrier((odd[3], total))
    pieces = odd_pieces(2, odd[2]) + odd_pieces(3, odd[3])
    if chips % 2:
        pieces += ends([odd[part][chips] for part in parts])
    return add(total, pieces, closes=True)


def solution(mesh):
    placed = (
        P("row", "col", None, None, None),
        P("row", "col", None),
        P("row", "col", None, None, None),
        P("row", "col", None),
        P("row", "col", None, None, None),
        P("row", "col", None),
        P("row", None),
    )
    return jax.shard_map(
        per_device, mesh=mesh, in_specs=placed, out_specs=P("row", "col"), check_vma=False
    )
```

```python
import functools

import jax
import jax.numpy as jnp
from jax import lax
from jax.experimental import pallas as pl
from jax.experimental.pallas import tpu as pltpu
from jax.sharding import PartitionSpec as P

CCOLS = 8
PARTS = 4
UNROLL = 16
HEAD = 16
VMEM_BYTES = 40 << 20
VMEM = pl.BlockSpec(memory_space=pltpu.VMEM)


def round_up(value, step):
    return value + -value % step


class Sizes:
    def __init__(self, n_stops, n_pairs, n_left, n_right, n_rows, n_col, edge):
        self.n_stops, self.n_pairs, self.n_rows, self.n_col = n_stops, n_pairs, n_rows, n_col
        self.n_left, self.n_right, self.edge = n_left, n_right, edge
        self.parts = PARTS
        self.per_part = n_right // PARTS
        self.zero_slot = n_col * n_left
        self.row_bits = (n_rows - 1).bit_length()
        self.key_bits = self.row_bits + (self.per_part - 1).bit_length()
        self.left_bits = self.zero_slot.bit_length()
        most = (n_pairs + self.per_part * n_rows) // 2
        self.width = round_up(round_up(most, UNROLL) + 1, 128)


def kernel_call(
    kernel,
    out_shape,
    operands,
    scalars=(),
    scratch=(),
    specs=None,
    out_space=pltpu.VMEM,
    vmem_bytes=VMEM_BYTES,
):
    return pl.pallas_call(
        kernel,
        out_shape=out_shape,
        grid_spec=pltpu.PrefetchScalarGridSpec(
            num_scalar_prefetch=len(scalars),
            in_specs=specs or [VMEM] * len(operands),
            out_specs=jax.tree.map(lambda _: pl.BlockSpec(memory_space=out_space), out_shape),
            scratch_shapes=list(scratch),
        ),
        compiler_params=pltpu.CompilerParams(vmem_limit_bytes=vmem_bytes),
        cost_estimate=pl.CostEstimate(flops=128, bytes_accessed=128, transcendentals=0),
    )(*scalars, *operands)


def pack_kernel(blocks_ref, ids_ref, *refs):
    part_refs, (got_ref, wide_ref, head_ref, sems) = refs[:-4], refs[-4:]
    rows = blocks_ref.shape[0] // len(part_refs)
    copies = [
        pltpu.make_async_copy(
            blocks_ref.at[pl.ds(part * rows, rows)], ref.at[pl.ds(HEAD, rows)], sems.at[part]
        )
        for part, ref in enumerate(part_refs)
    ]
    for copy in copies:
        copy.start()
    got = pltpu.make_async_copy(ids_ref, got_ref, sems.at[len(part_refs)])
    got.start()
    got.wait()
    wide_ref[...] = jnp.zeros_like(wide_ref)
    wide_ref[0:1, : ids_ref.shape[1]] = got_ref[...].astype(jnp.float32)
    head_ref[...] = wide_ref[...].astype(head_ref.dtype)
    heads = [
        pltpu.make_async_copy(
            head_ref, ref.at[pl.ds(0, HEAD)], sems.at[len(part_refs) + 1 + part]
        )
        for part, ref in enumerate(part_refs)
    ]
    for copy in heads:
        copy.start()
    for copy in copies + heads:
        copy.wait()


def pack(blocks, ids):
    edge = blocks.shape[-1]
    blocks, ids = blocks.reshape(-1, edge), ids.reshape(1, -1)
    shape = (HEAD + blocks.shape[0] // PARTS, edge)
    return kernel_call(
        pack_kernel,
        [jax.ShapeDtypeStruct(shape, blocks.dtype)] * PARTS,
        [blocks, ids],
        scratch=[
            pltpu.VMEM(ids.shape, ids.dtype),
            pltpu.VMEM((HEAD, edge), jnp.float32),
            pltpu.VMEM((HEAD, edge), blocks.dtype),
            pltpu.SemaphoreType.DMA((2 * PARTS + 1,)),
        ],
        specs=[pl.BlockSpec(memory_space=pl.ANY)] * 2,
        out_space=pl.ANY,
        vmem_bytes=60 << 20,
    )


def choose_kernel(*refs):
    parts = (len(refs) - 2) // 2
    out_ref, sems = refs[-2], refs[-1]
    rows = refs[0].shape[0]
    core = lax.rem(lax.axis_index("row"), 2)
    for which in range(2):

        @pl.when(core == which)
        def _(which=which):
            copies = [
                pltpu.make_async_copy(
                    refs[which * parts + part], out_ref.at[pl.ds(part * rows, rows)], sems.at[part]
                )
                for part in range(parts)
            ]
            for copy in copies:
                copy.start()
            for copy in copies:
                copy.wait()


def choose(lower, upper):
    rows, edge = lower[0].shape
    return kernel_call(
        choose_kernel,
        jax.ShapeDtypeStruct((len(lower) * rows, edge), lower[0].dtype),
        [*lower, *upper],
        scratch=[pltpu.SemaphoreType.DMA((len(lower),))],
        specs=[pl.BlockSpec(memory_space=pl.ANY)] * (2 * len(lower)),
    )


def ids_of(ref):
    return ref[:HEAD, :].astype(jnp.float32)[0:1, :]


def prepare_kernel(sizes, count_ref, order_ref, pairs_ref, *refs):
    id_refs, words_ref = refs[:-1], refs[-1]
    n_col, n_rows, parts = sizes.n_col, sizes.n_rows, sizes.parts
    n_pairs, width = sizes.n_pairs, sizes.width

    def total(mask, value, axis):
        return jnp.sum(jnp.where(mask, value, 0.0), axis=axis, keepdims=True)

    here = lax.axis_index("row")
    lane = lax.broadcasted_iota(jnp.int32, (n_pairs, 128), 1)
    slot = lax.broadcasted_iota(jnp.int32, (n_pairs, sizes.n_left), 1)
    down = lax.broadcasted_iota(jnp.int32, (n_pairs, 1), 0)
    across = lax.broadcasted_iota(jnp.int32, (1, n_pairs), 1)
    places = lax.broadcasted_iota(jnp.int32, (1, width), 1).astype(jnp.float32)
    dead = float(sizes.n_right * n_rows)
    lefts, keys = [], []
    key_matrix = jnp.zeros((n_pairs, 128), jnp.float32)
    for stop in range(sizes.n_stops):
        ahead = lax.rem(here + stop, n_col)
        ids = id_refs[0][...]
        for j in range(1, n_col):
            ids = jnp.where(ahead == j, id_refs[j][...], ids)
        left_row = jnp.zeros(ids.shape, jnp.float32)
        for i in range(n_rows):
            left_row = jnp.where(ids == i, order_ref[:, i : i + 1].astype(jnp.float32), left_row)
        left = pairs_ref[:, 2 * stop : 2 * stop + 1]
        right = pairs_ref[:, 2 * stop + 1 : 2 * stop + 2]
        key = right.astype(jnp.float32) * n_rows + total(slot == left, left_row, 1)
        key = jnp.where(down < count_ref[:, stop : stop + 1], key, dead)
        lefts.append((left + ahead * sizes.n_left - sizes.zero_slot).astype(jnp.float32))
        keys.append(key)
        key_matrix = jnp.where(lane == stop, key, key_matrix)
    key_rows = key_matrix.T
    cut = float(sizes.per_part * n_rows)

    def part_of(key):
        return sum(jnp.where(key >= part * cut, 1.0, 0.0) for part in range(1, parts))

    scale = [float(1 << sizes.key_bits), float(1 << (sizes.key_bits + sizes.left_bits))]
    empty = sizes.zero_slot * (scale[0] + scale[1])
    for stop in range(sizes.n_stops):
        left, key, other = lefts[stop], keys[stop], key_rows[stop : stop + 1, :]
        same = key == other
        rank = total(same & (across < down), 1.0, 1)
        other_rank = total(same & (down < across), 1.0, 0)
        other_opens = other_rank == 2.0 * jnp.floor(other_rank * 0.5)
        own_part, other_part = part_of(key), part_of(other)
        group = jnp.floor(rank * 0.5)
        opens = rank == 2.0 * group
        group += total((other < key) & (own_part == other_part) & other_opens, 1.0, 1)
        word = jnp.where(opens, left * scale[0] + key - own_part * cut, left * scale[1])
        for part in range(parts):
            counted = (own_part == float(part)) & (key < dead)
            words = empty + total(counted & (group == places), word, 0)
            words = jnp.where(places == width - 1.0, total(counted & opens, 1.0, 0), words)
            line = parts * stop + part
            words_ref[line : line + 1, :] = words.astype(jnp.int32)


def products_kernel(sizes, n_rights, layout, opens, closes, words_ref, *refs):
    n_sources = sizes.n_col if opens else 1
    sources, refs = refs[:n_sources], refs[n_sources:]
    right_refs, refs = refs[:n_rights], refs[n_rights:]
    start_ref = None
    if not opens:
        start_ref, refs = refs[0], refs[1:]
    out_ref, refs = refs[0], refs[1:]
    left_ref = sources[0]
    edge = sizes.edge
    if opens:
        left_ref, refs = refs[0], refs[1:]
        rows = sizes.n_left * edge
        for j, source in enumerate(sources):
            left_ref[j * rows : (j + 1) * rows, :] = source[...]
        left_ref[len(sources) * rows :, :] = jnp.zeros((edge, edge), left_ref.dtype)
    ids_ref, col_ref, copy_sem = refs[:3]
    total_ref = refs[3] if closes else out_ref
    for which, ref in enumerate(right_refs):
        ids_ref[which : which + 1, :] = ids_of(ref).astype(jnp.int32)
    copy = pltpu.make_async_copy(ids_ref, col_ref, copy_sem)
    copy.start()
    total_ref[...] = jnp.zeros_like(total_ref) if opens else start_ref[...]
    copy.wait()

    core, col = lax.rem(lax.axis_index("row"), 2), lax.axis_index("col")

    def block(ref, slot, head):
        return ref[pl.ds(pl.multiple_of(slot * edge + head, HEAD), edge), :]

    for array, head, part, ahead in layout:
        stop = jnp.where(
            core == 0,
            -1 if ahead[0] is None else ahead[0] - col,
            -1 if ahead[1] is None else ahead[1] - col,
        )
        used = (stop >= 0) & (stop < sizes.n_stops)
        line = jnp.clip(stop, 0, sizes.n_stops - 1) * sizes.parts + part
        count = jnp.where(used, words_ref[line, sizes.width - 1], 0)

        def groups(first, size, array=array, head=head, part=part, line=line):
            for member in range(size):
                word = words_ref[line, first + member]
                row = word & ((1 << sizes.row_bits) - 1)
                slot = (word & ((1 << sizes.key_bits) - 1)) >> sizes.row_bits
                word = word >> sizes.key_bits
                lefts = word & ((1 << sizes.left_bits) - 1), word >> sizes.left_bits
                target = row * CCOLS + col_ref[array, slot + part * sizes.per_part]
                right = block(right_refs[array], slot, head + HEAD)
                total_ref[target] += jnp.dot(
                    jnp.concatenate([block(left_ref, left, 0) for left in lefts], axis=1),
                    jnp.concatenate([right, right], axis=0),
                    preferred_element_type=jnp.float32,
                )

        steps = (count + UNROLL // 2 - 1) // UNROLL

        @pl.loop(0, steps)
        def _(step, groups=groups):
            groups(step * UNROLL, UNROLL)

        @pl.when(count > steps * UNROLL)
        def _(steps=steps, groups=groups):
            groups(steps * UNROLL, UNROLL // 2)

    if closes:
        for target in range(total_ref.shape[0]):
            row, col = divmod(target, CCOLS)
            out_ref[row * edge : (row + 1) * edge, col * edge : (col + 1) * edge] = total_ref[
                target
            ].astype(out_ref.dtype)


def per_device(a_blocks, a_rows, b_blocks, b_cols, pair_list, pair_count, row_order):
    n_row, n_col = lax.axis_size("row"), lax.axis_size("col")
    n_stops, n_pairs = pair_list.shape[2], pair_list.shape[4]
    sizes = Sizes(
        n_stops,
        n_pairs,
        a_blocks.shape[2],
        b_blocks.shape[2],
        row_order.shape[1],
        n_col,
        a_blocks.shape[3],
    )
    row = lax.axis_index("row")
    edge, sums = sizes.edge, (sizes.n_rows * CCOLS, sizes.edge, sizes.edge)
    reach = n_col + n_stops - 2
    chips = (reach + 1) // 2
    evens, odds = range(2, chips + 1, 2), range(1, chips + 1, 2)
    parts = range(PARTS)

    def from_ahead(block, axis, distance):
        size = lax.axis_size(axis)
        return lax.ppermute(block, axis, [((i + distance) % size, i) for i in range(size)])

    def swap(bit, lower, upper):
        mine = lower if lower is upper else jnp.where(row // bit % 2 == 1, upper, lower)
        return lax.ppermute(mine, "row", [(i ^ bit, i) for i in range(n_row)])

    def both(distance):
        return (distance, distance)

    def swapped(j):
        ahead = 2 * j + 1, 2 * j - 1
        return tuple(d if 1 <= d <= reach else None for d in ahead)

    left_ids = [a_rows.reshape(1, -1)]
    left_ids += [from_ahead(left_ids[0], "col", j) for j in range(1, n_col)]
    own = list(pack(b_blocks, b_cols))
    even = {j: [from_ahead(part, "row", 2 * j) for part in own] for j in range(2, chips + 2, 2)}
    left_own, left_ids = lax.optimization_barrier((a_blocks.reshape(-1, edge), left_ids))
    lefts = [left_own] + [from_ahead(left_own, "col", j) for j in range(1, n_col)]
    words = kernel_call(
        functools.partial(prepare_kernel, sizes),
        jax.ShapeDtypeStruct((PARTS * n_stops, sizes.width), jnp.int32),
        [pair_count.reshape(1, -1), row_order, pair_list.reshape(2 * n_stops, n_pairs).T]
        + left_ids,
    )

    def wait(part, *others):
        arrived, others = lax.optimization_barrier(([even[j][part] for j in even], others))
        for j, block in zip(even, arrived):
            even[j][part] = block
        return others

    def pass_on(part):
        sets = {0: own, **even}
        return {j: swap(2, sets[j + 1][part], sets[j - 1][part]) for j in odds}

    def add(total, pieces, closes=False):
        rights = list({id(piece[0]): piece[0] for piece in pieces}.values())
        places = {id(block): place for place, block in enumerate(rights)}
        layout = tuple((places[id(piece[0])], *piece[1:]) for piece in pieces)
        if closes:
            out_shape = jax.ShapeDtypeStruct((sizes.n_rows * edge, CCOLS * edge), jnp.bfloat16)
        else:
            out_shape = jax.ShapeDtypeStruct(sums, jnp.float32)
        if total is None:
            left_shape = ((sizes.zero_slot + 1) * edge, edge)
            out_shape = [out_shape, jax.ShapeDtypeStruct(left_shape, left_own.dtype)]
        lines = round_up(len(rights), 8)
        return kernel_call(
            functools.partial(
                products_kernel, sizes, len(rights), layout, total is None, closes
            ),
            out_shape,
            (lefts if total is None else [left_all])
            + rights
            + ([] if total is None else [total]),
            [words],
            [
                pltpu.VMEM((lines, 128), jnp.int32),
                pltpu.SMEM((lines, 128), jnp.int32),
                pltpu.SemaphoreType.DMA,
            ]
            + ([pltpu.VMEM(sums, jnp.float32)] if closes else []),
        )

    def pieces_of(j, part, block):
        pieces = [(block, 0, part, both(2 * j))]
        if j < chips:
            pieces.append((swap(1, block, block), 0, part, swapped(j)))
        return pieces

    def odd_pieces(part, sets):
        return [piece for j in odds for piece in pieces_of(j, part, sets[j])]

    def ends(sets):
        chosen = choose(sets, own)
        arrived = swap(1, chosen, chosen)
        ahead = swapped(0)[0], swapped(chips)[1]
        rows = own[0].shape[0]
        return [(arrived, part * rows, part, ahead) for part in parts]

    odd = {}
    (words,) = wait(0, words)
    odd[0] = pass_on(0)
    (lefts,) = wait(1, lefts)
    odd[1] = pass_on(1)
    total, left_all = add(None, [(own[part], 0, part, both(0)) for part in parts])
    odd[0], odd[1], total = wait(2, odd[0], odd[1], total)
    odd[2] = pass_on(2)
    pieces = odd_pieces(0, odd[0]) + odd_pieces(1, odd[1])
    total = add(total, pieces)
    odd[2], total = wait(3, odd[2], total)
    odd[3] = pass_on(3)
    pieces = [piece for j in evens for part in parts for piece in pieces_of(j, part, even[j][part])]
    if chips % 2 == 0:
        pieces += ends(even[chips])
    total = add(total, pieces)
    odd[3], total = lax.optimization_barrier((odd[3], total))
    pieces = odd_pieces(2, odd[2]) + odd_pieces(3, odd[3])
    if chips % 2:
        pieces += ends([odd[part][chips] for part in parts])
    return add(total, pieces, closes=True)


def solution(mesh):
    placed = (
        P("row", "col", None, None, None),
        P("row", "col", None),
        P("row", "col", None, None, None),
        P("row", "col", None),
        P("row", "col", None, None, None),
        P("row", "col", None),
        P("row", None),
    )
    return jax.shard_map(
        per_device, mesh=mesh, in_specs=placed, out_specs=P("row", "col"), check_vma=False
    )
```

```python
import functools

import jax
import jax.numpy as jnp
from jax import lax
from jax.experimental import pallas as pl
from jax.experimental.pallas import tpu as pltpu
from jax.sharding import PartitionSpec as P

CCOLS = 8
PARTS = 2
UNROLL = 16
HEAD = 16
VMEM_BYTES = 40 << 20
VMEM = pl.BlockSpec(memory_space=pltpu.VMEM)


def round_up(value, step):
    return value + -value % step


class Sizes:
    def __init__(self, n_stops, n_pairs, n_left, n_right, n_rows, n_col, edge):
        self.n_stops, self.n_pairs, self.n_rows, self.n_col = n_stops, n_pairs, n_rows, n_col
        self.n_left, self.n_right, self.edge = n_left, n_right, edge
        self.parts = PARTS
        self.per_part = n_right // PARTS
        self.zero_slot = n_col * n_left
        self.row_bits = (n_rows - 1).bit_length()
        self.key_bits = self.row_bits + (self.per_part - 1).bit_length()
        self.left_bits = self.zero_slot.bit_length()
        most = (n_pairs + self.per_part * n_rows) // 2
        self.width = round_up(round_up(most, UNROLL) + 1, 128)


def kernel_call(
    kernel,
    out_shape,
    operands,
    scalars=(),
    scratch=(),
    specs=None,
):
    return pl.pallas_call(
        kernel,
        out_shape=out_shape,
        grid_spec=pltpu.PrefetchScalarGridSpec(
            num_scalar_prefetch=len(scalars),
            in_specs=specs or [VMEM] * len(operands),
            out_specs=jax.tree.map(lambda _: VMEM, out_shape),
            scratch_shapes=list(scratch),
        ),
        compiler_params=pltpu.CompilerParams(vmem_limit_bytes=VMEM_BYTES),
        cost_estimate=pl.CostEstimate(flops=128, bytes_accessed=128, transcendentals=0),
    )(*scalars, *operands)


def pack_kernel(blocks_ref, ids_ref, *refs):
    part_refs, head_ref, sems = refs[:-2], refs[-2], refs[-1]
    rows = blocks_ref.shape[0] // len(part_refs)
    copies = [
        pltpu.make_async_copy(
            blocks_ref.at[pl.ds(part * rows, rows)], ref.at[pl.ds(HEAD, rows)], sems.at[part]
        )
        for part, ref in enumerate(part_refs)
    ]
    for copy in copies:
        copy.start()
    head_ref[...] = jnp.zeros_like(head_ref)
    head_ref[0:1, : ids_ref.shape[1]] = ids_ref[...].astype(jnp.float32)
    for ref in part_refs:
        ref[:HEAD, :] = head_ref[...].astype(ref.dtype)
    for copy in copies:
        copy.wait()


def pack(blocks, ids):
    edge = blocks.shape[-1]
    blocks = blocks.reshape(-1, edge)
    shape = (HEAD + blocks.shape[0] // PARTS, edge)
    return kernel_call(
        pack_kernel,
        [jax.ShapeDtypeStruct(shape, blocks.dtype)] * PARTS,
        [blocks, ids.reshape(1, -1)],
        scratch=[pltpu.VMEM((HEAD, edge), jnp.float32), pltpu.SemaphoreType.DMA((PARTS,))],
        specs=[pl.BlockSpec(memory_space=pl.ANY), VMEM],
    )


def ids_of(ref):
    return ref[:HEAD, :].astype(jnp.float32)[0:1, :]


def prepare_kernel(sizes, count_ref, order_ref, pairs_ref, *refs):
    id_refs, words_ref = refs[:-1], refs[-1]
    n_col, n_rows, parts = sizes.n_col, sizes.n_rows, sizes.parts
    n_pairs, width = sizes.n_pairs, sizes.width

    def total(mask, value, axis):
        return jnp.sum(jnp.where(mask, value, 0.0), axis=axis, keepdims=True)

    here = lax.axis_index("row")
    lane = lax.broadcasted_iota(jnp.int32, (n_pairs, 128), 1)
    slot = lax.broadcasted_iota(jnp.int32, (n_pairs, sizes.n_left), 1)
    down = lax.broadcasted_iota(jnp.int32, (n_pairs, 1), 0)
    across = lax.broadcasted_iota(jnp.int32, (1, n_pairs), 1)
    places = lax.broadcasted_iota(jnp.int32, (1, width), 1).astype(jnp.float32)
    dead = float(sizes.n_right * n_rows)
    lefts, keys = [], []
    key_matrix = jnp.zeros((n_pairs, 128), jnp.float32)
    for stop in range(sizes.n_stops):
        ahead = lax.rem(here + stop, n_col)
        ids = id_refs[0][...]
        for j in range(1, n_col):
            ids = jnp.where(ahead == j, id_refs[j][...], ids)
        left_row = jnp.zeros(ids.shape, jnp.float32)
        for i in range(n_rows):
            left_row = jnp.where(ids == i, order_ref[:, i : i + 1].astype(jnp.float32), left_row)
        left = pairs_ref[:, 2 * stop : 2 * stop + 1]
        right = pairs_ref[:, 2 * stop + 1 : 2 * stop + 2]
        key = right.astype(jnp.float32) * n_rows + total(slot == left, left_row, 1)
        key = jnp.where(down < count_ref[:, stop : stop + 1], key, dead)
        lefts.append((left + ahead * sizes.n_left - sizes.zero_slot).astype(jnp.float32))
        keys.append(key)
        key_matrix = jnp.where(lane == stop, key, key_matrix)
    key_rows = key_matrix.T
    cut = float(sizes.per_part * n_rows)

    def part_of(key):
        return sum(jnp.where(key >= part * cut, 1.0, 0.0) for part in range(1, parts))

    scale = [float(1 << sizes.key_bits), float(1 << (sizes.key_bits + sizes.left_bits))]
    empty = sizes.zero_slot * (scale[0] + scale[1])
    for stop in range(sizes.n_stops):
        left, key, other = lefts[stop], keys[stop], key_rows[stop : stop + 1, :]
        same = key == other
        rank = total(same & (across < down), 1.0, 1)
        other_rank = total(same & (down < across), 1.0, 0)
        other_opens = other_rank == 2.0 * jnp.floor(other_rank * 0.5)
        own_part, other_part = part_of(key), part_of(other)
        group = jnp.floor(rank * 0.5)
        opens = rank == 2.0 * group
        group += total((other < key) & (own_part == other_part) & other_opens, 1.0, 1)
        word = jnp.where(opens, left * scale[0] + key - own_part * cut, left * scale[1])
        for part in range(parts):
            counted = (own_part == float(part)) & (key < dead)
            words = empty + total(counted & (group == places), word, 0)
            words = jnp.where(places == width - 1.0, total(counted & opens, 1.0, 0), words)
            line = parts * stop + part
            words_ref[line : line + 1, :] = words.astype(jnp.int32)


def products_kernel(sizes, n_rights, layout, opens, closes, words_ref, *refs):
    n_sources = sizes.n_col if opens else 1
    sources, refs = refs[:n_sources], refs[n_sources:]
    right_refs, refs = refs[:n_rights], refs[n_rights:]
    start_ref = None
    if not opens:
        start_ref, refs = refs[0], refs[1:]
    out_ref, refs = refs[0], refs[1:]
    left_ref = sources[0]
    edge = sizes.edge
    if opens:
        left_ref, refs = refs[0], refs[1:]
        rows = sizes.n_left * edge
        for j, source in enumerate(sources):
            left_ref[j * rows : (j + 1) * rows, :] = source[...]
        left_ref[len(sources) * rows :, :] = jnp.zeros((edge, edge), left_ref.dtype)
    ids_ref, col_ref, copy_sem = refs[:3]
    total_ref = refs[3] if closes else out_ref
    for which, ref in enumerate(right_refs):
        ids_ref[which : which + 1, :] = ids_of(ref).astype(jnp.int32)
    copy = pltpu.make_async_copy(ids_ref, col_ref, copy_sem)
    copy.start()
    total_ref[...] = jnp.zeros_like(total_ref) if opens else start_ref[...]
    copy.wait()

    core, col = lax.rem(lax.axis_index("row"), 2), lax.axis_index("col")

    def block(ref, slot, head):
        return ref[pl.ds(pl.multiple_of(slot * edge + head, HEAD), edge), :]

    for array, head, part, ahead in layout:
        stop = jnp.where(
            core == 0,
            -1 if ahead[0] is None else ahead[0] - col,
            -1 if ahead[1] is None else ahead[1] - col,
        )
        used = (stop >= 0) & (stop < sizes.n_stops)
        line = jnp.clip(stop, 0, sizes.n_stops - 1) * sizes.parts + part
        count = jnp.where(used, words_ref[line, sizes.width - 1], 0)

        def groups(first, size, array=array, head=head, part=part, line=line):
            for member in range(size):
                word = words_ref[line, first + member]
                row = word & ((1 << sizes.row_bits) - 1)
                slot = (word & ((1 << sizes.key_bits) - 1)) >> sizes.row_bits
                word = word >> sizes.key_bits
                lefts = word & ((1 << sizes.left_bits) - 1), word >> sizes.left_bits
                target = row * CCOLS + col_ref[array, slot + part * sizes.per_part]
                right = block(right_refs[array], slot, head + HEAD)
                total_ref[target] += jnp.dot(
                    jnp.concatenate([block(left_ref, left, 0) for left in lefts], axis=1),
                    jnp.concatenate([right, right], axis=0),
                    preferred_element_type=jnp.float32,
                )

        steps = (count + UNROLL // 2 - 1) // UNROLL

        @pl.loop(0, steps)
        def _(step, groups=groups):
            groups(step * UNROLL, UNROLL)

        @pl.when(count > steps * UNROLL)
        def _(steps=steps, groups=groups):
            groups(steps * UNROLL, UNROLL // 2)

    if closes:
        for target in range(total_ref.shape[0]):
            row, col = divmod(target, CCOLS)
            out_ref[row * edge : (row + 1) * edge, col * edge : (col + 1) * edge] = total_ref[
                target
            ].astype(out_ref.dtype)


def per_device(a_blocks, a_rows, b_blocks, b_cols, pair_list, pair_count, row_order):
    n_row, n_col = lax.axis_size("row"), lax.axis_size("col")
    n_stops, n_pairs = pair_list.shape[2], pair_list.shape[4]
    sizes = Sizes(
        n_stops,
        n_pairs,
        a_blocks.shape[2],
        b_blocks.shape[2],
        row_order.shape[1],
        n_col,
        a_blocks.shape[3],
    )
    row = lax.axis_index("row")
    edge, sums = sizes.edge, (sizes.n_rows * CCOLS, sizes.edge, sizes.edge)
    reach = n_col + n_stops - 2
    chips = (reach + 1) // 2
    evens, odds = range(2, chips + 1, 2), range(1, chips + 1, 2)
    parts = range(PARTS)

    def from_ahead(block, axis, distance):
        size = lax.axis_size(axis)
        return lax.ppermute(block, axis, [((i + distance) % size, i) for i in range(size)])

    def swap(bit, lower, upper):
        mine = lower if lower is upper else jnp.where(row // bit % 2 == 1, upper, lower)
        return lax.ppermute(mine, "row", [(i ^ bit, i) for i in range(n_row)])

    def both(distance):
        return (distance, distance)

    def swapped(j):
        ahead = 2 * j + 1, 2 * j - 1
        return tuple(d if 1 <= d <= reach else None for d in ahead)

    left_ids = [a_rows.reshape(1, -1)]
    left_ids += [from_ahead(left_ids[0], "col", j) for j in range(1, n_col)]
    own = list(pack(b_blocks, b_cols))
    even = {j: [from_ahead(part, "row", 2 * j) for part in own] for j in range(2, chips + 2, 2)}
    left_own, left_ids = lax.optimization_barrier((a_blocks.reshape(-1, edge), left_ids))
    lefts = [left_own] + [from_ahead(left_own, "col", j) for j in range(1, n_col)]
    words = kernel_call(
        functools.partial(prepare_kernel, sizes),
        jax.ShapeDtypeStruct((PARTS * n_stops, sizes.width), jnp.int32),
        [pair_count.reshape(1, -1), row_order, pair_list.reshape(2 * n_stops, n_pairs).T]
        + left_ids,
    )

    def wait(part, *others):
        arrived, others = lax.optimization_barrier(([even[j][part] for j in even], others))
        for j, block in zip(even, arrived):
            even[j][part] = block
        return others

    def pass_on(part):
        sets = {0: own, **even}
        return {j: swap(2, sets[j + 1][part], sets[j - 1][part]) for j in odds}

    def add(total, pieces, closes=False):
        rights = list({id(piece[0]): piece[0] for piece in pieces}.values())
        places = {id(block): place for place, block in enumerate(rights)}
        layout = tuple((places[id(piece[0])], *piece[1:]) for piece in pieces)
        if closes:
            out_shape = jax.ShapeDtypeStruct((sizes.n_rows * edge, CCOLS * edge), jnp.bfloat16)
        else:
            out_shape = jax.ShapeDtypeStruct(sums, jnp.float32)
        if total is None:
            left_shape = ((sizes.zero_slot + 1) * edge, edge)
            out_shape = [out_shape, jax.ShapeDtypeStruct(left_shape, left_own.dtype)]
        lines = round_up(len(rights), 8)
        return kernel_call(
            functools.partial(
                products_kernel, sizes, len(rights), layout, total is None, closes
            ),
            out_shape,
            (lefts if total is None else [left_all])
            + rights
            + ([] if total is None else [total]),
            [words],
            [
                pltpu.VMEM((lines, 128), jnp.int32),
                pltpu.SMEM((lines, 128), jnp.int32),
                pltpu.SemaphoreType.DMA,
            ]
            + ([pltpu.VMEM(sums, jnp.float32)] if closes else []),
        )

    def pieces_of(j, part, block):
        pieces = [(block, 0, part, both(2 * j))]
        if j < chips:
            pieces.append((swap(1, block, block), 0, part, swapped(j)))
        return pieces

    def odd_pieces(part):
        return [piece for j in odds for piece in pieces_of(j, part, odd[part][j])]

    def even_pieces(part):
        return [piece for j in evens for piece in pieces_of(j, part, even[j][part])]

    def end_pieces(part):
        farthest = odd[part][chips] if chips % 2 else even[chips][part]
        ahead = swapped(0)[0], swapped(chips)[1]
        return [(swap(1, farthest, own[part]), 0, part, ahead)]

    def even_and_end(parts):
        pieces = []
        for part in parts:
            pieces += even_pieces(part) + ([] if chips % 2 else end_pieces(part))
        return pieces

    def odd_and_end(parts):
        pieces = []
        for part in parts:
            pieces += odd_pieces(part) + (end_pieces(part) if chips % 2 else [])
        return pieces

    odd = {}
    words, lefts = wait(0, words, lefts)
    odd[0] = pass_on(0)
    pieces = [(own[part], 0, part, both(0)) for part in parts]
    total, left_all = add(None, pieces + even_pieces(0))
    odd[0], total = wait(1, odd[0], total)
    odd[1] = pass_on(1)
    ends = [] if chips % 2 else end_pieces(0)
    total = add(total, odd_and_end((0,)) + ends + even_and_end((1,)))
    odd[1], total = lax.optimization_barrier((odd[1], total))
    return add(total, odd_and_end((1,)), closes=True)


def solution(mesh):
    placed = (
        P("row", "col", None, None, None),
        P("row", "col", None),
        P("row", "col", None, None, None),
        P("row", "col", None),
        P("row", "col", None, None, None),
        P("row", "col", None),
        P("row", None),
    )
    return jax.shard_map(
        per_device, mesh=mesh, in_specs=placed, out_specs=P("row", "col"), check_vma=False
    )
```

```python
import functools

import jax
import jax.numpy as jnp
from jax import lax
from jax.experimental import pallas as pl
from jax.experimental.pallas import tpu as pltpu
from jax.sharding import PartitionSpec as P

CCOLS = 8
PARTS = 2
UNROLL = 16
HEADS = (16, 32)
VMEM_BYTES = 40 << 20
VMEM = pl.BlockSpec(memory_space=pltpu.VMEM)


def round_up(value, step):
    return value + -value % step


class Sizes:
    def __init__(self, n_stops, n_pairs, n_left, n_right, n_rows, n_col, edge):
        self.n_stops, self.n_pairs, self.n_rows, self.n_col = n_stops, n_pairs, n_rows, n_col
        self.n_left, self.n_right, self.edge = n_left, n_right, edge
        self.parts = PARTS
        self.per_part = n_right // PARTS
        self.zero_slot = n_col * n_left
        self.row_bits = (n_rows - 1).bit_length()
        self.key_bits = self.row_bits + (self.per_part - 1).bit_length()
        self.left_bits = self.zero_slot.bit_length()
        most = (n_pairs + self.per_part * n_rows) // 2
        self.width = round_up(round_up(most, UNROLL) + 1, 128)


def kernel_call(
    kernel,
    out_shape,
    operands,
    scalars=(),
    scratch=(),
    specs=None,
):
    return pl.pallas_call(
        kernel,
        out_shape=out_shape,
        grid_spec=pltpu.PrefetchScalarGridSpec(
            num_scalar_prefetch=len(scalars),
            in_specs=specs or [VMEM] * len(operands),
            out_specs=jax.tree.map(lambda _: VMEM, out_shape),
            scratch_shapes=list(scratch),
        ),
        compiler_params=pltpu.CompilerParams(vmem_limit_bytes=VMEM_BYTES),
        cost_estimate=pl.CostEstimate(flops=128, bytes_accessed=128, transcendentals=0),
    )(*scalars, *operands)


def pack_kernel(layout, *refs):
    block_refs, id_refs = refs[: len(layout)], refs[len(layout) : 2 * len(layout)]
    part_refs, (head_ref, sems) = list(refs[2 * len(layout) : -2]), refs[-2:]
    copies, heads = [], []
    for (parts, block_ref, ids_ref) in zip(layout, block_refs, id_refs):
        for low, count, head in parts:
            ref = part_refs[len(copies)]
            source, target = block_ref.at[pl.ds(low, count)], ref.at[pl.ds(head, count)]
            copies.append(pltpu.make_async_copy(source, target, sems.at[len(copies)]))
            heads.append((ref, head, ids_ref))
    for copy in copies:
        copy.start()
    for ref, head, ids_ref in heads:
        head_ref[...] = jnp.zeros_like(head_ref)
        head_ref[0:1, : ids_ref.shape[1]] = ids_ref[...].astype(jnp.float32)
        for row in range(0, head, 16):
            ref[row : row + 16, :] = head_ref[...].astype(ref.dtype)
    for copy in copies:
        copy.wait()


def pack(edge, sets):
    layout, shapes = [], []
    for blocks, _, heads in sets:
        rows = blocks.shape[0] // len(heads)
        layout.append(tuple((part * rows, rows, head) for part, head in enumerate(heads)))
        shapes += [jax.ShapeDtypeStruct((head + rows, edge), blocks.dtype) for head in heads]
    return kernel_call(
        functools.partial(pack_kernel, tuple(layout)),
        shapes,
        [blocks for blocks, _, _ in sets] + [ids.reshape(1, -1) for _, ids, _ in sets],
        scratch=[pltpu.VMEM((16, edge), jnp.float32), pltpu.SemaphoreType.DMA((len(shapes),))],
        specs=[pl.BlockSpec(memory_space=pl.ANY)] * len(sets) + [VMEM] * len(sets),
    )


def ids_of(ref):
    return ref[:16, :].astype(jnp.float32)[0:1, :]


def prepare_kernel(sizes, count_ref, order_ref, pairs_ref, *refs):
    words_ref = refs[-1]
    id_sets = [ids_of(ref) for ref in refs[:-1]]
    n_col, n_rows, parts = sizes.n_col, sizes.n_rows, sizes.parts
    n_pairs, width = sizes.n_pairs, sizes.width

    def total(mask, value, axis):
        return jnp.sum(jnp.where(mask, value, 0.0), axis=axis, keepdims=True)

    here = lax.axis_index("row")
    lane = lax.broadcasted_iota(jnp.int32, (n_pairs, 128), 1)
    down = lax.broadcasted_iota(jnp.int32, (n_pairs, 1), 0)
    across = lax.broadcasted_iota(jnp.int32, (1, n_pairs), 1)
    places = lax.broadcasted_iota(jnp.int32, (1, width), 1).astype(jnp.float32)
    dead = float(sizes.n_right * n_rows)
    lefts, keys = [], []
    key_matrix = jnp.zeros((n_pairs, 128), jnp.float32)
    for stop in range(sizes.n_stops):
        ahead = lax.rem(here + stop, n_col)
        ids = id_sets[0]
        for j in range(1, n_col):
            ids = jnp.where(ahead == j, id_sets[j], ids)
        left_row = jnp.zeros(ids.shape, jnp.float32)
        for i in range(n_rows):
            left_row = jnp.where(ids == float(i), order_ref[:, i : i + 1].astype(jnp.float32), left_row)
        left = pairs_ref[:, 2 * stop : 2 * stop + 1]
        right = pairs_ref[:, 2 * stop + 1 : 2 * stop + 2]
        key = right.astype(jnp.float32) * n_rows + total(lane == left, left_row, 1)
        key = jnp.where(down < count_ref[:, stop : stop + 1], key, dead)
        lefts.append((left + ahead * sizes.n_left - sizes.zero_slot).astype(jnp.float32))
        keys.append(key)
        key_matrix = jnp.where(lane == stop, key, key_matrix)
    key_rows = key_matrix.T
    cut = float(sizes.per_part * n_rows)

    def part_of(key):
        return sum(jnp.where(key >= part * cut, 1.0, 0.0) for part in range(1, parts))

    scale = [float(1 << sizes.key_bits), float(1 << (sizes.key_bits + sizes.left_bits))]
    empty = sizes.zero_slot * (scale[0] + scale[1])
    for stop in range(sizes.n_stops):
        left, key, other = lefts[stop], keys[stop], key_rows[stop : stop + 1, :]
        same = key == other
        rank = total(same & (across < down), 1.0, 1)
        other_rank = total(same & (down < across), 1.0, 0)
        other_opens = other_rank == 2.0 * jnp.floor(other_rank * 0.5)
        own_part, other_part = part_of(key), part_of(other)
        group = jnp.floor(rank * 0.5)
        opens = rank == 2.0 * group
        group += total((other < key) & (own_part == other_part) & other_opens, 1.0, 1)
        word = jnp.where(opens, left * scale[0] + key - own_part * cut, left * scale[1])
        for part in range(parts):
            counted = (own_part == float(part)) & (key < dead)
            words = empty + total(counted & (group == places), word, 0)
            words = jnp.where(places == width - 1.0, total(counted & opens, 1.0, 0), words)
            line = parts * stop + part
            words_ref[line : line + 1, :] = words.astype(jnp.int32)


def products_kernel(sizes, n_rights, layout, opens, closes, words_ref, *refs):
    n_sources = sizes.n_col if opens else 1
    sources, refs = refs[:n_sources], refs[n_sources:]
    right_refs, refs = refs[:n_rights], refs[n_rights:]
    start_ref = None
    if not opens:
        start_ref, refs = refs[0], refs[1:]
    out_ref, refs = refs[0], refs[1:]
    left_ref = sources[0]
    edge = sizes.edge
    if opens:
        left_ref, refs = refs[0], refs[1:]
        rows = sizes.n_left * edge
        for j, source in enumerate(sources):
            left_ref[j * rows : (j + 1) * rows, :] = source[HEADS[-1] :, :]
        left_ref[len(sources) * rows :, :] = jnp.zeros((edge, edge), left_ref.dtype)
    ids_ref, col_ref, copy_sem = refs[:3]
    total_ref = refs[3] if closes else out_ref
    for which, ref in enumerate(right_refs):
        ids_ref[which : which + 1, :] = ids_of(ref).astype(jnp.int32)
    copy = pltpu.make_async_copy(ids_ref, col_ref, copy_sem)
    copy.start()
    total_ref[...] = jnp.zeros_like(total_ref) if opens else start_ref[...]
    copy.wait()

    core, col = lax.rem(lax.axis_index("row"), 2), lax.axis_index("col")

    def block(ref, slot, head):
        return ref[pl.ds(pl.multiple_of(slot * edge + head, 16), edge), :]

    for array, head, part, ahead in layout:
        stop = jnp.where(
            core == 0,
            -1 if ahead[0] is None else ahead[0] - col,
            -1 if ahead[1] is None else ahead[1] - col,
        )
        used = (stop >= 0) & (stop < sizes.n_stops)
        line = jnp.clip(stop, 0, sizes.n_stops - 1) * sizes.parts + part
        count = jnp.where(used, words_ref[line, sizes.width - 1], 0)

        def groups(first, size, array=array, head=head, part=part, line=line):
            for member in range(size):
                word = words_ref[line, first + member]
                row = word & ((1 << sizes.row_bits) - 1)
                slot = (word & ((1 << sizes.key_bits) - 1)) >> sizes.row_bits
                word = word >> sizes.key_bits
                lefts = word & ((1 << sizes.left_bits) - 1), word >> sizes.left_bits
                target = row * CCOLS + col_ref[array, slot + part * sizes.per_part]
                right = block(right_refs[array], slot, head)
                total_ref[target] += jnp.dot(
                    jnp.concatenate([block(left_ref, left, 0) for left in lefts], axis=1),
                    jnp.concatenate([right, right], axis=0),
                    preferred_element_type=jnp.float32,
                )

        steps = (count + UNROLL // 2 - 1) // UNROLL

        @pl.loop(0, steps)
        def _(step, groups=groups):
            groups(step * UNROLL, UNROLL)

        @pl.when(count > steps * UNROLL)
        def _(steps=steps, groups=groups):
            groups(steps * UNROLL, UNROLL // 2)

    if closes:
        for target in range(total_ref.shape[0]):
            row, col = divmod(target, CCOLS)
            out_ref[row * edge : (row + 1) * edge, col * edge : (col + 1) * edge] = total_ref[
                target
            ].astype(out_ref.dtype)


def per_device(a_blocks, a_rows, b_blocks, b_cols, pair_list, pair_count, row_order):
    n_row, n_col = lax.axis_size("row"), lax.axis_size("col")
    n_stops, n_pairs = pair_list.shape[2], pair_list.shape[4]
    sizes = Sizes(
        n_stops,
        n_pairs,
        a_blocks.shape[2],
        b_blocks.shape[2],
        row_order.shape[1],
        n_col,
        a_blocks.shape[3],
    )
    row = lax.axis_index("row")
    edge, sums = sizes.edge, (sizes.n_rows * CCOLS, sizes.edge, sizes.edge)
    reach = n_col + n_stops - 2
    chips = (reach + 1) // 2
    evens, odds = range(2, chips + 1, 2), range(1, chips + 1, 2)
    parts = range(PARTS)

    def from_ahead(block, axis, distance):
        size = lax.axis_size(axis)
        return lax.ppermute(block, axis, [((i + distance) % size, i) for i in range(size)])

    def swap(bit, lower, upper, skip=0):
        mine = lower if lower is upper else jnp.where(row // bit % 2 == 1, upper, lower)
        mine = mine[skip:]
        return lax.ppermute(mine, "row", [(i ^ bit, i) for i in range(n_row)])

    def both(distance):
        return (distance, distance)

    def swapped(j):
        ahead = 2 * j + 1, 2 * j - 1
        return tuple(d if 1 <= d <= reach else None for d in ahead)

    right_blocks, left_blocks = b_blocks.reshape(-1, edge), a_blocks.reshape(-1, edge)
    *own, left_own = pack(
        edge, [(right_blocks, b_cols, HEADS), (left_blocks, a_rows, HEADS[-1:])]
    )
    even = {j: [from_ahead(part, "row", 2 * j) for part in own] for j in range(2, chips + 2, 2)}
    lefts = [left_own] + [from_ahead(left_own, "col", j) for j in range(1, n_col)]
    def wait(part, *others):
        arrived, others = lax.optimization_barrier(([even[j][part] for j in even], others))
        for j, block in zip(even, arrived):
            even[j][part] = block
        return others

    def pass_on(part):
        sets = {0: own, **even}
        return {j: swap(2, sets[j + 1][part], sets[j - 1][part]) for j in odds}

    def add(total, pieces, closes=False):
        rights = list({id(piece[0]): piece[0] for piece in pieces}.values())
        places = {id(block): place for place, block in enumerate(rights)}
        layout = tuple((places[id(piece[0])], *piece[1:]) for piece in pieces)
        if closes:
            out_shape = jax.ShapeDtypeStruct((sizes.n_rows * edge, CCOLS * edge), jnp.bfloat16)
        else:
            out_shape = jax.ShapeDtypeStruct(sums, jnp.float32)
        if total is None:
            left_shape = ((sizes.zero_slot + 1) * edge, edge)
            out_shape = [out_shape, jax.ShapeDtypeStruct(left_shape, b_blocks.dtype)]
        lines = round_up(len(rights), 8)
        return kernel_call(
            functools.partial(
                products_kernel, sizes, len(rights), layout, total is None, closes
            ),
            out_shape,
            (lefts if total is None else [left_all])
            + rights
            + ([] if total is None else [total]),
            [words],
            [
                pltpu.VMEM((lines, 128), jnp.int32),
                pltpu.SMEM((lines, 128), jnp.int32),
                pltpu.SemaphoreType.DMA,
            ]
            + ([pltpu.VMEM(sums, jnp.float32)] if closes else []),
        )

    def pieces_of(j, part, block):
        head = HEADS[part]
        pieces = [(block, head, part, both(2 * j))]
        if j < chips:
            pieces.append((swap(1, block, block), head, part, swapped(j)))
        return pieces

    def odd_pieces(part):
        return [piece for j in odds for piece in pieces_of(j, part, odd[part][j])]

    def even_pieces(part):
        return [piece for j in evens for piece in pieces_of(j, part, even[j][part])]

    def end_pieces(part):
        farthest = odd[part][chips] if chips % 2 else even[chips][part]
        ahead = swapped(0)[0], swapped(chips)[1]
        extra = HEADS[part] - HEADS[0]
        return [(swap(1, farthest, own[part], extra), HEADS[0], part, ahead)]

    def even_and_end(parts):
        pieces = []
        for part in parts:
            pieces += even_pieces(part) + ([] if chips % 2 else end_pieces(part))
        return pieces

    def odd_and_end(parts):
        pieces = []
        for part in parts:
            pieces += odd_pieces(part) + (end_pieces(part) if chips % 2 else [])
        return pieces

    odd = {}
    (lefts,) = wait(0, lefts)
    odd[0] = pass_on(0)
    words = kernel_call(
        functools.partial(prepare_kernel, sizes),
        jax.ShapeDtypeStruct((PARTS * n_stops, sizes.width), jnp.int32),
        [pair_count.reshape(1, -1), row_order, pair_list.reshape(2 * n_stops, n_pairs).T]
        + lefts,
    )
    pieces = [(own[part], HEADS[part], part, both(0)) for part in parts]
    total, left_all = add(None, pieces + even_pieces(0))
    odd[0], total = wait(1, odd[0], total)
    odd[1] = pass_on(1)
    ends = [] if chips % 2 else end_pieces(0)
    total = add(total, odd_and_end((0,)) + ends + even_and_end((1,)))
    odd[1], total = lax.optimization_barrier((odd[1], total))
    return add(total, odd_and_end((1,)), closes=True)


def solution(mesh):
    placed = (
        P("row", "col", None, None, None),
        P("row", "col", None),
        P("row", "col", None, None, None),
        P("row", "col", None),
        P("row", "col", None, None, None),
        P("row", "col", None),
        P("row", None),
    )
    return jax.shard_map(
        per_device, mesh=mesh, in_specs=placed, out_specs=P("row", "col"), check_vma=False
    )
```

```python
import functools

import jax
import jax.numpy as jnp
from jax import lax
from jax.experimental import pallas as pl
from jax.experimental.pallas import tpu as pltpu
from jax.sharding import PartitionSpec as P

CCOLS = 8
PARTS = 2
FIRST_PART = 15, 32
UNROLL = 16
HEAD = 32
HEAD_STEP = 16
VMEM_BYTES = 40 << 20
VMEM = pl.BlockSpec(memory_space=pltpu.VMEM)


def round_up(value, step):
    return value + -value % step


class Sizes:
    def __init__(self, n_stops, n_pairs, n_left, n_right, n_rows, n_col, edge):
        self.n_stops, self.n_pairs, self.n_rows, self.n_col = n_stops, n_pairs, n_rows, n_col
        self.n_left, self.n_right, self.edge = n_left, n_right, edge
        self.parts = PARTS
        first = n_right * FIRST_PART[0] // FIRST_PART[1]
        self.cuts = (0, first, n_right)
        self.per_part = max(first, n_right - first)
        self.zero_slot = n_col * n_left
        self.row_bits = (n_rows - 1).bit_length()
        self.key_bits = self.row_bits + (self.per_part - 1).bit_length()
        self.left_bits = self.zero_slot.bit_length()
        most = (n_pairs + self.per_part * n_rows) // 2
        self.width = round_up(round_up(most, UNROLL) + 1, 128)


def kernel_call(
    kernel,
    out_shape,
    operands,
    scalars=(),
    scratch=(),
    specs=None,
    flops=128,
):
    return pl.pallas_call(
        kernel,
        out_shape=out_shape,
        grid_spec=pltpu.PrefetchScalarGridSpec(
            num_scalar_prefetch=len(scalars),
            in_specs=specs or [VMEM] * len(operands),
            out_specs=jax.tree.map(lambda _: VMEM, out_shape),
            scratch_shapes=list(scratch),
        ),
        compiler_params=pltpu.CompilerParams(vmem_limit_bytes=VMEM_BYTES),
        cost_estimate=pl.CostEstimate(flops=flops, bytes_accessed=128, transcendentals=0),
    )(*scalars, *operands)


def pack_kernel(cuts, blocks_ref, ids_ref, *refs):
    part_refs, head_ref, sems = refs[:-2], refs[-2], refs[-1]
    edge = blocks_ref.shape[1]
    copies = []
    for part, ref in enumerate(part_refs):
        low, count = cuts[part] * edge, (cuts[part + 1] - cuts[part]) * edge
        source, target = blocks_ref.at[pl.ds(low, count)], ref.at[pl.ds(HEAD, count)]
        copies.append(pltpu.make_async_copy(source, target, sems.at[part]))
    for copy in copies:
        copy.start()
    head_ref[...] = jnp.zeros_like(head_ref)
    head_ref[0:1, : ids_ref.shape[1]] = ids_ref[...].astype(jnp.float32)
    for ref in part_refs:
        for row in range(0, HEAD, HEAD_STEP):
            ref[row : row + HEAD_STEP, :] = head_ref[...].astype(ref.dtype)
    for copy in copies:
        copy.wait()


def pack(sizes, blocks, ids):
    edge = sizes.edge
    counts = [high - low for low, high in zip(sizes.cuts, sizes.cuts[1:])]
    shapes = [(HEAD + count * edge, edge) for count in counts]
    return kernel_call(
        functools.partial(pack_kernel, sizes.cuts),
        [jax.ShapeDtypeStruct(shape, blocks.dtype) for shape in shapes],
        [blocks.reshape(-1, edge), ids.reshape(1, -1)],
        scratch=[pltpu.VMEM((HEAD_STEP, edge), jnp.float32), pltpu.SemaphoreType.DMA((PARTS,))],
        specs=[pl.BlockSpec(memory_space=pl.ANY), VMEM],
    )


def ids_of(ref):
    return ref[:HEAD_STEP, :].astype(jnp.float32)[0:1, :]


def prepare_kernel(sizes, count_ref, order_ref, pairs_ref, *refs):
    words_ref = refs[-1]
    id_sets = [ref[...] for ref in refs[:-1]]
    n_col, n_rows, parts = sizes.n_col, sizes.n_rows, sizes.parts
    n_pairs, width = sizes.n_pairs, sizes.width

    def total(mask, value, axis):
        return jnp.sum(jnp.where(mask, value, 0.0), axis=axis, keepdims=True)

    here = lax.axis_index("row")
    lane = lax.broadcasted_iota(jnp.int32, (n_pairs, 128), 1)
    slot = lane[:, : sizes.n_left]
    down = lax.broadcasted_iota(jnp.int32, (n_pairs, 1), 0)
    across = lax.broadcasted_iota(jnp.int32, (1, n_pairs), 1)
    places = lax.broadcasted_iota(jnp.int32, (1, width), 1).astype(jnp.float32)
    dead = float(sizes.n_right * n_rows)
    lefts, keys = [], []
    key_matrix = jnp.zeros((n_pairs, 128), jnp.float32)
    for stop in range(sizes.n_stops):
        ahead = lax.rem(here + stop, n_col)
        ids = id_sets[0]
        for j in range(1, n_col):
            ids = jnp.where(ahead == j, id_sets[j], ids)
        left_row = jnp.zeros(ids.shape, jnp.float32)
        for i in range(n_rows):
            left_row = jnp.where(ids == i, order_ref[:, i : i + 1].astype(jnp.float32), left_row)
        left = pairs_ref[:, 2 * stop : 2 * stop + 1]
        right = pairs_ref[:, 2 * stop + 1 : 2 * stop + 2]
        key = right.astype(jnp.float32) * n_rows + total(slot == left, left_row, 1)
        key = jnp.where(down < count_ref[:, stop : stop + 1], key, dead)
        lefts.append((left + ahead * sizes.n_left - sizes.zero_slot).astype(jnp.float32))
        keys.append(key)
        key_matrix = jnp.where(lane == stop, key, key_matrix)
    key_rows = key_matrix.T
    cut = float(sizes.cuts[1] * n_rows)

    def part_of(key):
        return jnp.where(key >= cut, 1.0, 0.0)

    scale = [float(1 << sizes.key_bits), float(1 << (sizes.key_bits + sizes.left_bits))]
    empty = sizes.zero_slot * (scale[0] + scale[1])
    for stop in range(sizes.n_stops):
        left, key, other = lefts[stop], keys[stop], key_rows[stop : stop + 1, :]
        same = key == other
        rank = total(same & (across < down), 1.0, 1)
        other_rank = total(same & (down < across), 1.0, 0)
        other_opens = other_rank == 2.0 * jnp.floor(other_rank * 0.5)
        own_part, other_part = part_of(key), part_of(other)
        group = jnp.floor(rank * 0.5)
        opens = rank == 2.0 * group
        group += total((other < key) & (own_part == other_part) & other_opens, 1.0, 1)
        word = jnp.where(opens, left * scale[0] + key - own_part * cut, left * scale[1])
        for part in range(parts):
            counted = (own_part == float(part)) & (key < dead)
            words = empty + total(counted & (group == places), word, 0)
            words = jnp.where(places == width - 1.0, total(counted & opens, 1.0, 0), words)
            line = parts * stop + part
            words_ref[line : line + 1, :] = words.astype(jnp.int32)


def products_kernel(sizes, n_rights, layout, opens, closes, words_ref, *refs):
    n_sources = sizes.n_col if opens else 1
    sources, refs = refs[:n_sources], refs[n_sources:]
    right_refs, refs = refs[:n_rights], refs[n_rights:]
    start_ref = None
    if not opens:
        start_ref, refs = refs[0], refs[1:]
    out_ref, refs = refs[0], refs[1:]
    left_ref = sources[0]
    edge = sizes.edge
    if opens:
        left_ref, refs = refs[0], refs[1:]
        rows = sizes.n_left * edge
        for j, source in enumerate(sources):
            left_ref[j * rows : (j + 1) * rows, :] = source[...]
        left_ref[len(sources) * rows :, :] = jnp.zeros((edge, edge), left_ref.dtype)
    ids_ref, col_ref, copy_sem = refs[:3]
    total_ref = refs[3] if closes else out_ref
    for which, ref in enumerate(right_refs):
        ids_ref[which : which + 1, :] = ids_of(ref).astype(jnp.int32)
    copy = pltpu.make_async_copy(ids_ref, col_ref, copy_sem)
    copy.start()
    total_ref[...] = jnp.zeros_like(total_ref) if opens else start_ref[...]
    copy.wait()

    core, col = lax.rem(lax.axis_index("row"), 2), lax.axis_index("col")

    def block(ref, slot, head):
        return ref[pl.ds(pl.multiple_of(slot * edge + head, HEAD_STEP), edge), :]

    for array, head, part, ahead in layout:
        stop = jnp.where(
            core == 0,
            -1 if ahead[0] is None else ahead[0] - col,
            -1 if ahead[1] is None else ahead[1] - col,
        )
        used = (stop >= 0) & (stop < sizes.n_stops)
        line = jnp.clip(stop, 0, sizes.n_stops - 1) * sizes.parts + part
        count = jnp.where(used, words_ref[line, sizes.width - 1], 0)

        def groups(first, size, array=array, head=head, part=part, line=line):
            for member in range(size):
                word = words_ref[line, first + member]
                row = word & ((1 << sizes.row_bits) - 1)
                slot = (word & ((1 << sizes.key_bits) - 1)) >> sizes.row_bits
                word = word >> sizes.key_bits
                lefts = word & ((1 << sizes.left_bits) - 1), word >> sizes.left_bits
                target = row * CCOLS + col_ref[array, slot + sizes.cuts[part]]
                right = block(right_refs[array], slot, head)
                total_ref[target] += jnp.dot(
                    jnp.concatenate([block(left_ref, left, 0) for left in lefts], axis=1),
                    jnp.concatenate([right, right], axis=0),
                    preferred_element_type=jnp.float32,
                )

        steps = (count + UNROLL // 2 - 1) // UNROLL

        @pl.loop(0, steps)
        def _(step, groups=groups):
            groups(step * UNROLL, UNROLL)

        @pl.when(count > steps * UNROLL)
        def _(steps=steps, groups=groups):
            groups(steps * UNROLL, UNROLL // 2)

    if closes:
        for target in range(total_ref.shape[0]):
            row, col = divmod(target, CCOLS)
            out_ref[row * edge : (row + 1) * edge, col * edge : (col + 1) * edge] = total_ref[
                target
            ].astype(out_ref.dtype)


def per_device(a_blocks, a_rows, b_blocks, b_cols, pair_list, pair_count, row_order):
    n_row, n_col = lax.axis_size("row"), lax.axis_size("col")
    n_stops, n_pairs = pair_list.shape[2], pair_list.shape[4]
    sizes = Sizes(
        n_stops,
        n_pairs,
        a_blocks.shape[2],
        b_blocks.shape[2],
        row_order.shape[1],
        n_col,
        a_blocks.shape[3],
    )
    row = lax.axis_index("row")
    edge, sums = sizes.edge, (sizes.n_rows * CCOLS, sizes.edge, sizes.edge)
    reach = n_col + n_stops - 2
    chips = (reach + 1) // 2
    evens, odds = range(2, chips + 1, 2), range(1, chips + 1, 2)
    parts = range(PARTS)

    def from_ahead(block, axis, distance):
        size = lax.axis_size(axis)
        return lax.ppermute(block, axis, [((i + distance) % size, i) for i in range(size)])

    def swap(bit, lower, upper, skip=0):
        mine = lower if lower is upper else jnp.where(row // bit % 2 == 1, upper, lower)
        mine = mine[skip:]
        return lax.ppermute(mine, "row", [(i ^ bit, i) for i in range(n_row)])

    def both(distance):
        return (distance, distance)

    def swapped(j):
        ahead = 2 * j + 1, 2 * j - 1
        return tuple(d if 1 <= d <= reach else None for d in ahead)

    own = pack(sizes, b_blocks, b_cols)
    even = {j: [from_ahead(part, "row", 2 * j) for part in own] for j in range(2, chips + 2, 2)}
    left_ids, left_own = a_rows.reshape(1, -1), a_blocks.reshape(-1, edge)
    left_ids = [left_ids] + [from_ahead(left_ids, "col", j) for j in range(1, n_col)]
    lefts = [left_own] + [from_ahead(left_own, "col", j) for j in range(1, n_col)]
    words = kernel_call(
        functools.partial(prepare_kernel, sizes),
        jax.ShapeDtypeStruct((PARTS * n_stops, sizes.width), jnp.int32),
        [pair_count.reshape(1, -1), row_order, pair_list.reshape(2 * n_stops, n_pairs).T]
        + left_ids,
        flops=1 << 34,
    )

    def wait(part, *others):
        arrived, others = lax.optimization_barrier(([even[j][part] for j in even], others))
        for j, block in zip(even, arrived):
            even[j][part] = block
        return others

    def pass_on(part):
        sets = {0: own, **even}
        return {j: swap(2, sets[j + 1][part], sets[j - 1][part]) for j in odds}

    def add(total, pieces, closes=False):
        rights = list({id(piece[0]): piece[0] for piece in pieces}.values())
        places = {id(block): place for place, block in enumerate(rights)}
        layout = tuple((places[id(piece[0])], *piece[1:]) for piece in pieces)
        if closes:
            out_shape = jax.ShapeDtypeStruct((sizes.n_rows * edge, CCOLS * edge), jnp.bfloat16)
        else:
            out_shape = jax.ShapeDtypeStruct(sums, jnp.float32)
        if total is None:
            left_shape = ((sizes.zero_slot + 1) * edge, edge)
            out_shape = [out_shape, jax.ShapeDtypeStruct(left_shape, b_blocks.dtype)]
        lines = round_up(len(rights), 8)
        return kernel_call(
            functools.partial(
                products_kernel, sizes, len(rights), layout, total is None, closes
            ),
            out_shape,
            (lefts if total is None else [left_all])
            + rights
            + ([] if total is None else [total]),
            [words],
            [
                pltpu.VMEM((lines, 128), jnp.int32),
                pltpu.SMEM((lines, 128), jnp.int32),
                pltpu.SemaphoreType.DMA,
            ]
            + ([pltpu.VMEM(sums, jnp.float32)] if closes else []),
        )

    def pieces_of(j, part, block):
        skip = HEAD_STEP if j in evens else 0
        theirs = swap(1, block, block, skip)
        return [
            (block, HEAD, part, both(2 * j)),
            (theirs, HEAD - skip, part, swapped(j)),
        ]

    odd = {}
    words, lefts = wait(0, words, lefts)
    odd[0] = pass_on(0)
    pieces = [piece for part in parts for piece in pieces_of(0, part, own[part])]
    pieces += [piece for j in evens for piece in pieces_of(j, 0, even[j][0])]
    total, left_all = add(None, pieces)
    odd[0], total = wait(1, odd[0], total)
    odd[1] = pass_on(1)
    pieces = [piece for j in odds for piece in pieces_of(j, 0, odd[0][j])]
    pieces += [piece for j in evens for piece in pieces_of(j, 1, even[j][1])]
    total = add(total, pieces)
    odd[1], total = lax.optimization_barrier((odd[1], total))
    pieces = [piece for j in odds for piece in pieces_of(j, 1, odd[1][j])]
    return add(total, pieces, closes=True)


def solution(mesh):
    placed = (
        P("row", "col", None, None, None),
        P("row", "col", None),
        P("row", "col", None, None, None),
        P("row", "col", None),
        P("row", "col", None, None, None),
        P("row", "col", None),
        P("row", None),
    )
    return jax.shard_map(
        per_device, mesh=mesh, in_specs=placed, out_specs=P("row", "col"), check_vma=False
    )
```

```python
import functools

import jax
import jax.numpy as jnp
from jax import lax
from jax.experimental import pallas as pl
from jax.experimental.pallas import tpu as pltpu
from jax.sharding import PartitionSpec as P

CCOLS = 8
PARTS = 2
FIRST_PART = 15, 32
UNROLL = 16
HEAD = 32
HEAD_STEP = 16
VMEM_BYTES = 40 << 20
VMEM = pl.BlockSpec(memory_space=pltpu.VMEM)


def round_up(value, step):
    return value + -value % step


class Sizes:
    def __init__(self, n_stops, n_pairs, n_left, n_right, n_rows, n_col, edge):
        self.n_stops, self.n_pairs, self.n_rows, self.n_col = n_stops, n_pairs, n_rows, n_col
        self.n_left, self.n_right, self.edge = n_left, n_right, edge
        self.parts = PARTS
        first = n_right * FIRST_PART[0] // FIRST_PART[1]
        self.cuts = (0, first, n_right)
        self.per_part = max(first, n_right - first)
        self.zero_slot = n_col * n_left
        self.row_bits = (n_rows - 1).bit_length()
        self.key_bits = self.row_bits + (self.per_part - 1).bit_length()
        self.left_bits = self.zero_slot.bit_length()
        most = (n_pairs + self.per_part * n_rows) // 2
        self.width = round_up(round_up(most, UNROLL) + 1, 128)


def kernel_call(
    kernel,
    out_shape,
    operands,
    scalars=(),
    scratch=(),
    specs=None,
    vmem_bytes=VMEM_BYTES,
):
    return pl.pallas_call(
        kernel,
        out_shape=out_shape,
        grid_spec=pltpu.PrefetchScalarGridSpec(
            num_scalar_prefetch=len(scalars),
            in_specs=specs or [VMEM] * len(operands),
            out_specs=jax.tree.map(lambda _: VMEM, out_shape),
            scratch_shapes=list(scratch),
        ),
        compiler_params=pltpu.CompilerParams(vmem_limit_bytes=vmem_bytes),
        cost_estimate=pl.CostEstimate(flops=128, bytes_accessed=128, transcendentals=0),
    )(*scalars, *operands)


def pack_kernel(layout, *refs):
    n_sets = len(layout)
    block_refs, id_refs, refs = refs[:n_sets], refs[n_sets : 2 * n_sets], refs[2 * n_sets :]
    head_ref, sems, refs = refs[-2], refs[-1], list(refs[:-2])
    copies, heads = [], []
    for cuts, blocks_ref, ids_ref in zip(layout, block_refs, id_refs):
        for low, high in zip(cuts, cuts[1:]):
            ref = refs.pop(0)
            source, target = blocks_ref.at[pl.ds(low, high - low)], ref.at[pl.ds(HEAD, high - low)]
            copies.append(pltpu.make_async_copy(source, target, sems.at[len(copies)]))
            copies[-1].start()
            heads.append((ref, ids_ref))
    for ref, ids_ref in heads:
        head_ref[...] = jnp.zeros_like(head_ref)
        head_ref[0:1, : ids_ref.shape[1]] = ids_ref[...].astype(jnp.float32)
        for row in range(0, HEAD, HEAD_STEP):
            ref[row : row + HEAD_STEP, :] = head_ref[...].astype(ref.dtype)
    for copy in copies:
        copy.wait()


def pack(sets):
    shapes = []
    for blocks, _, cuts in sets:
        for low, high in zip(cuts, cuts[1:]):
            shapes.append(jax.ShapeDtypeStruct((HEAD + high - low, blocks.shape[1]), blocks.dtype))
    edge = shapes[0].shape[1]
    return kernel_call(
        functools.partial(pack_kernel, tuple(cuts for _, _, cuts in sets)),
        shapes,
        [blocks for blocks, _, _ in sets] + [ids for _, ids, _ in sets],
        scratch=[
            pltpu.VMEM((HEAD_STEP, edge), jnp.float32),
            pltpu.SemaphoreType.DMA((len(shapes),)),
        ],
        specs=[pl.BlockSpec(memory_space=pl.ANY)] * len(sets) + [VMEM] * len(sets),
        vmem_bytes=60 << 20,
    )


def ids_of(ref):
    return ref[:HEAD_STEP, :].astype(jnp.float32)[0:1, :]


def prepare_kernel(sizes, count_ref, order_ref, pairs_ref, *refs):
    words_ref = refs[-1]
    id_sets = [ids_of(ref) for ref in refs[:-1]]
    n_col, n_rows, parts = sizes.n_col, sizes.n_rows, sizes.parts
    n_pairs, width = sizes.n_pairs, sizes.width

    def total(mask, value, axis):
        return jnp.sum(jnp.where(mask, value, 0.0), axis=axis, keepdims=True)

    here = lax.axis_index("row")
    lane = lax.broadcasted_iota(jnp.int32, (n_pairs, 128), 1)
    down = lax.broadcasted_iota(jnp.int32, (n_pairs, 1), 0)
    across = lax.broadcasted_iota(jnp.int32, (1, n_pairs), 1)
    places = lax.broadcasted_iota(jnp.int32, (1, width), 1).astype(jnp.float32)
    dead = float(sizes.n_right * n_rows)
    lefts, keys = [], []
    key_matrix = jnp.zeros((n_pairs, 128), jnp.float32)
    for stop in range(sizes.n_stops):
        ahead = lax.rem(here + stop, n_col)
        ids = id_sets[0]
        for j in range(1, n_col):
            ids = jnp.where(ahead == j, id_sets[j], ids)
        left_row = jnp.zeros(ids.shape, jnp.float32)
        for i in range(n_rows):
            left_row = jnp.where(ids == float(i), order_ref[:, i : i + 1].astype(jnp.float32), left_row)
        left = pairs_ref[:, 2 * stop : 2 * stop + 1]
        right = pairs_ref[:, 2 * stop + 1 : 2 * stop + 2]
        key = right.astype(jnp.float32) * n_rows + total(lane == left, left_row, 1)
        key = jnp.where(down < count_ref[:, stop : stop + 1], key, dead)
        lefts.append((left + ahead * sizes.n_left - sizes.zero_slot).astype(jnp.float32))
        keys.append(key)
        key_matrix = jnp.where(lane == stop, key, key_matrix)
    key_rows = key_matrix.T
    cut = float(sizes.cuts[1] * n_rows)

    def part_of(key):
        return jnp.where(key >= cut, 1.0, 0.0)

    scale = [float(1 << sizes.key_bits), float(1 << (sizes.key_bits + sizes.left_bits))]
    empty = sizes.zero_slot * (scale[0] + scale[1])
    for stop in range(sizes.n_stops):
        left, key, other = lefts[stop], keys[stop], key_rows[stop : stop + 1, :]
        same = key == other
        rank = total(same & (across < down), 1.0, 1)
        other_rank = total(same & (down < across), 1.0, 0)
        other_opens = other_rank == 2.0 * jnp.floor(other_rank * 0.5)
        own_part, other_part = part_of(key), part_of(other)
        group = jnp.floor(rank * 0.5)
        opens = rank == 2.0 * group
        group += total((other < key) & (own_part == other_part) & other_opens, 1.0, 1)
        word = jnp.where(opens, left * scale[0] + key - own_part * cut, left * scale[1])
        for part in range(parts):
            counted = (own_part == float(part)) & (key < dead)
            words = empty + total(counted & (group == places), word, 0)
            words = jnp.where(places == width - 1.0, total(counted & opens, 1.0, 0), words)
            line = parts * stop + part
            words_ref[line : line + 1, :] = words.astype(jnp.int32)


def products_kernel(sizes, n_rights, layout, opens, closes, words_ref, *refs):
    n_sources = sizes.n_col if opens else 1
    sources, refs = refs[:n_sources], refs[n_sources:]
    right_refs, refs = refs[:n_rights], refs[n_rights:]
    start_ref = None
    if not opens:
        start_ref, refs = refs[0], refs[1:]
    out_ref, refs = refs[0], refs[1:]
    left_ref = sources[0]
    edge = sizes.edge
    if opens:
        left_ref, refs = refs[0], refs[1:]
        rows = sizes.n_left * edge
        for j, source in enumerate(sources):
            left_ref[j * rows : (j + 1) * rows, :] = source[HEAD:, :]
        left_ref[len(sources) * rows :, :] = jnp.zeros((edge, edge), left_ref.dtype)
    ids_ref, col_ref, copy_sem = refs[:3]
    total_ref = refs[3] if closes else out_ref
    for which, ref in enumerate(right_refs):
        ids_ref[which : which + 1, :] = ids_of(ref).astype(jnp.int32)
    copy = pltpu.make_async_copy(ids_ref, col_ref, copy_sem)
    copy.start()
    total_ref[...] = jnp.zeros_like(total_ref) if opens else start_ref[...]
    copy.wait()

    core, col = lax.rem(lax.axis_index("row"), 2), lax.axis_index("col")

    def block(ref, slot, head):
        return ref[pl.ds(pl.multiple_of(slot * edge + head, HEAD_STEP), edge), :]

    for array, head, part, ahead in layout:
        stop = jnp.where(
            core == 0,
            -1 if ahead[0] is None else ahead[0] - col,
            -1 if ahead[1] is None else ahead[1] - col,
        )
        used = (stop >= 0) & (stop < sizes.n_stops)
        line = jnp.clip(stop, 0, sizes.n_stops - 1) * sizes.parts + part
        count = jnp.where(used, words_ref[line, sizes.width - 1], 0)

        def groups(first, size, array=array, head=head, part=part, line=line):
            for member in range(size):
                word = words_ref[line, first + member]
                row = word & ((1 << sizes.row_bits) - 1)
                slot = (word & ((1 << sizes.key_bits) - 1)) >> sizes.row_bits
                word = word >> sizes.key_bits
                lefts = word & ((1 << sizes.left_bits) - 1), word >> sizes.left_bits
                target = row * CCOLS + col_ref[array, slot + sizes.cuts[part]]
                right = block(right_refs[array], slot, head)
                total_ref[target] += jnp.dot(
                    jnp.concatenate([block(left_ref, left, 0) for left in lefts], axis=1),
                    jnp.concatenate([right, right], axis=0),
                    preferred_element_type=jnp.float32,
                )

        steps = (count + UNROLL // 2 - 1) // UNROLL

        @pl.loop(0, steps)
        def _(step, groups=groups):
            groups(step * UNROLL, UNROLL)

        @pl.when(count > steps * UNROLL)
        def _(steps=steps, groups=groups):
            groups(steps * UNROLL, UNROLL // 2)

    if closes:
        for target in range(total_ref.shape[0]):
            row, col = divmod(target, CCOLS)
            out_ref[row * edge : (row + 1) * edge, col * edge : (col + 1) * edge] = total_ref[
                target
            ].astype(out_ref.dtype)


def per_device(a_blocks, a_rows, b_blocks, b_cols, pair_list, pair_count, row_order):
    n_row, n_col = lax.axis_size("row"), lax.axis_size("col")
    n_stops, n_pairs = pair_list.shape[2], pair_list.shape[4]
    sizes = Sizes(
        n_stops,
        n_pairs,
        a_blocks.shape[2],
        b_blocks.shape[2],
        row_order.shape[1],
        n_col,
        a_blocks.shape[3],
    )
    row = lax.axis_index("row")
    edge, sums = sizes.edge, (sizes.n_rows * CCOLS, sizes.edge, sizes.edge)
    reach = n_col + n_stops - 2
    chips = (reach + 1) // 2
    evens, odds = range(2, chips + 1, 2), range(1, chips + 1, 2)
    parts = range(PARTS)

    def from_ahead(block, axis, distance):
        size = lax.axis_size(axis)
        return lax.ppermute(block, axis, [((i + distance) % size, i) for i in range(size)])

    def swap(bit, lower, upper, skip=0):
        mine = lower if lower is upper else jnp.where(row // bit % 2 == 1, upper, lower)
        mine = mine[skip:]
        return lax.ppermute(mine, "row", [(i ^ bit, i) for i in range(n_row)])

    def both(distance):
        return (distance, distance)

    def swapped(j):
        ahead = 2 * j + 1, 2 * j - 1
        return tuple(d if 1 <= d <= reach else None for d in ahead)

    rights = b_blocks.reshape(-1, edge), b_cols.reshape(1, -1), [cut * edge for cut in sizes.cuts]
    lefts = a_blocks.reshape(-1, edge), a_rows.reshape(1, -1), [0, sizes.n_left * edge]
    *own, left_own = pack([rights, lefts])
    even = {j: [from_ahead(part, "row", 2 * j) for part in own] for j in range(2, chips + 2, 2)}
    lefts = [left_own] + [from_ahead(left_own, "col", j) for j in range(1, n_col)]

    def wait(part, *others):
        arrived, others = lax.optimization_barrier(([even[j][part] for j in even], others))
        for j, block in zip(even, arrived):
            even[j][part] = block
        return others

    def pass_on(part):
        sets = {0: own, **even}
        return {j: swap(2, sets[j + 1][part], sets[j - 1][part]) for j in odds}

    def add(total, pieces, closes=False):
        rights = list({id(piece[0]): piece[0] for piece in pieces}.values())
        places = {id(block): place for place, block in enumerate(rights)}
        layout = tuple((places[id(piece[0])], *piece[1:]) for piece in pieces)
        if closes:
            out_shape = jax.ShapeDtypeStruct((sizes.n_rows * edge, CCOLS * edge), jnp.bfloat16)
        else:
            out_shape = jax.ShapeDtypeStruct(sums, jnp.float32)
        if total is None:
            left_shape = ((sizes.zero_slot + 1) * edge, edge)
            out_shape = [out_shape, jax.ShapeDtypeStruct(left_shape, b_blocks.dtype)]
        lines = round_up(len(rights), 8)
        return kernel_call(
            functools.partial(
                products_kernel, sizes, len(rights), layout, total is None, closes
            ),
            out_shape,
            (lefts if total is None else [left_all])
            + rights
            + ([] if total is None else [total]),
            [words],
            [
                pltpu.VMEM((lines, 128), jnp.int32),
                pltpu.SMEM((lines, 128), jnp.int32),
                pltpu.SemaphoreType.DMA,
            ]
            + ([pltpu.VMEM(sums, jnp.float32)] if closes else []),
        )

    def pieces_of(j, part, block):
        skip = HEAD_STEP if j in evens else 0
        theirs = swap(1, block, block, skip)
        return [
            (block, HEAD, part, both(2 * j)),
            (theirs, HEAD - skip, part, swapped(j)),
        ]

    odd = {}
    (lefts,) = wait(0, lefts)
    odd[0] = pass_on(0)
    words = kernel_call(
        functools.partial(prepare_kernel, sizes),
        jax.ShapeDtypeStruct((PARTS * n_stops, sizes.width), jnp.int32),
        [pair_count.reshape(1, -1), row_order, pair_list.reshape(2 * n_stops, n_pairs).T]
        + lefts,
    )
    pieces = [piece for part in parts for piece in pieces_of(0, part, own[part])]
    pieces += [piece for j in evens for piece in pieces_of(j, 0, even[j][0])]
    total, left_all = add(None, pieces)
    odd[0], total = wait(1, odd[0], total)
    odd[1] = pass_on(1)
    pieces = [piece for j in odds for piece in pieces_of(j, 0, odd[0][j])]
    pieces += [piece for j in evens for piece in pieces_of(j, 1, even[j][1])]
    total = add(total, pieces)
    odd[1], total = lax.optimization_barrier((odd[1], total))
    pieces = [piece for j in odds for piece in pieces_of(j, 1, odd[1][j])]
    return add(total, pieces, closes=True)


def solution(mesh):
    placed = (
        P("row", "col", None, None, None),
        P("row", "col", None),
        P("row", "col", None, None, None),
        P("row", "col", None),
        P("row", "col", None, None, None),
        P("row", "col", None),
        P("row", None),
    )
    return jax.shard_map(
        per_device, mesh=mesh, in_specs=placed, out_specs=P("row", "col"), check_vma=False
    )
```

```python
import functools

import jax
import jax.numpy as jnp
from jax import lax
from jax.experimental import pallas as pl
from jax.experimental.pallas import tpu as pltpu
from jax.sharding import PartitionSpec as P

CCOLS = 8
PARTS = 2
FIRST_PART = 15, 32
UNROLL = 16
HEAD = 32
HEAD_STEP = 16
VMEM_BYTES = 40 << 20
VMEM = pl.BlockSpec(memory_space=pltpu.VMEM)


def round_up(value, step):
    return value + -value % step


class Sizes:
    def __init__(self, n_stops, n_pairs, n_left, n_right, n_rows, n_col, edge):
        self.n_stops, self.n_pairs, self.n_rows, self.n_col = n_stops, n_pairs, n_rows, n_col
        self.n_left, self.n_right, self.edge = n_left, n_right, edge
        self.parts = PARTS
        first = n_right * FIRST_PART[0] // FIRST_PART[1]
        self.cuts = (0, first, n_right)
        self.per_part = max(first, n_right - first)
        self.zero_slot = n_col * n_left
        self.row_bits = (n_rows - 1).bit_length()
        self.key_bits = self.row_bits + (self.per_part - 1).bit_length()
        self.left_bits = self.zero_slot.bit_length()
        most = (n_pairs + self.per_part * n_rows) // 2
        self.width = round_up(round_up(most, UNROLL) + 1, 128)


def kernel_call(
    kernel,
    out_shape,
    operands,
    scalars=(),
    scratch=(),
    specs=None,
    flops=128,
):
    return pl.pallas_call(
        kernel,
        out_shape=out_shape,
        grid_spec=pltpu.PrefetchScalarGridSpec(
            num_scalar_prefetch=len(scalars),
            in_specs=specs or [VMEM] * len(operands),
            out_specs=jax.tree.map(lambda _: VMEM, out_shape),
            scratch_shapes=list(scratch),
        ),
        compiler_params=pltpu.CompilerParams(vmem_limit_bytes=VMEM_BYTES),
        cost_estimate=pl.CostEstimate(flops=flops, bytes_accessed=128, transcendentals=0),
    )(*scalars, *operands)


def pack_kernel(cuts, blocks_ref, ids_ref, *refs):
    part_refs, head_ref, sems = refs[:-2], refs[-2], refs[-1]
    edge = blocks_ref.shape[1]
    copies = []
    for part, ref in enumerate(part_refs):
        low, count = cuts[part] * edge, (cuts[part + 1] - cuts[part]) * edge
        source, target = blocks_ref.at[pl.ds(low, count)], ref.at[pl.ds(HEAD, count)]
        copies.append(pltpu.make_async_copy(source, target, sems.at[part]))
    for copy in copies:
        copy.start()
    head_ref[...] = jnp.zeros_like(head_ref)
    head_ref[0:1, : ids_ref.shape[1]] = ids_ref[...].astype(jnp.float32)
    for ref in part_refs:
        for row in range(0, HEAD, HEAD_STEP):
            ref[row : row + HEAD_STEP, :] = head_ref[...].astype(ref.dtype)
    for copy in copies:
        copy.wait()


def pack(sizes, blocks, ids):
    edge = sizes.edge
    counts = [high - low for low, high in zip(sizes.cuts, sizes.cuts[1:])]
    shapes = [(HEAD + count * edge, edge) for count in counts]
    return kernel_call(
        functools.partial(pack_kernel, sizes.cuts),
        [jax.ShapeDtypeStruct(shape, blocks.dtype) for shape in shapes],
        [blocks.reshape(-1, edge), ids.reshape(1, -1)],
        scratch=[pltpu.VMEM((HEAD_STEP, edge), jnp.float32), pltpu.SemaphoreType.DMA((PARTS,))],
        specs=[pl.BlockSpec(memory_space=pl.ANY), VMEM],
    )


def ids_of(ref):
    return ref[:HEAD_STEP, :].astype(jnp.float32)[0:1, :]


def prepare_kernel(sizes, count_ref, order_ref, pairs_ref, *refs):
    words_ref = refs[-1]
    id_sets = [ref[...] for ref in refs[:-1]]
    n_col, n_rows, parts = sizes.n_col, sizes.n_rows, sizes.parts
    n_pairs, width = sizes.n_pairs, sizes.width

    def total(mask, value, axis):
        return jnp.sum(jnp.where(mask, value, 0.0), axis=axis, keepdims=True)

    here = lax.axis_index("row")
    lane = lax.broadcasted_iota(jnp.int32, (n_pairs, 128), 1)
    slot = lane[:, : sizes.n_left]
    down = lax.broadcasted_iota(jnp.int32, (n_pairs, 1), 0)
    across = lax.broadcasted_iota(jnp.int32, (1, n_pairs), 1)
    places = lax.broadcasted_iota(jnp.int32, (1, width), 1).astype(jnp.float32)
    dead = float(sizes.n_right * n_rows)
    lefts, keys = [], []
    key_matrix = jnp.zeros((n_pairs, 128), jnp.float32)
    for stop in range(sizes.n_stops):
        ahead = lax.rem(here + stop, n_col)
        ids = id_sets[0]
        for j in range(1, n_col):
            ids = jnp.where(ahead == j, id_sets[j], ids)
        left_row = jnp.zeros(ids.shape, jnp.float32)
        for i in range(n_rows):
            left_row = jnp.where(ids == i, order_ref[:, i : i + 1].astype(jnp.float32), left_row)
        left = pairs_ref[:, 2 * stop : 2 * stop + 1]
        right = pairs_ref[:, 2 * stop + 1 : 2 * stop + 2]
        key = right.astype(jnp.float32) * n_rows + total(slot == left, left_row, 1)
        key = jnp.where(down < count_ref[:, stop : stop + 1], key, dead)
        lefts.append((left + ahead * sizes.n_left - sizes.zero_slot).astype(jnp.float32))
        keys.append(key)
        key_matrix = jnp.where(lane == stop, key, key_matrix)
    key_rows = key_matrix.T
    cut = float(sizes.cuts[1] * n_rows)

    def part_of(key):
        return jnp.where(key >= cut, 1.0, 0.0)

    scale = [float(1 << sizes.key_bits), float(1 << (sizes.key_bits + sizes.left_bits))]
    empty = sizes.zero_slot * (scale[0] + scale[1])
    for stop in range(sizes.n_stops):
        left, key, other = lefts[stop], keys[stop], key_rows[stop : stop + 1, :]
        same = key == other
        rank = total(same & (across < down), 1.0, 1)
        other_rank = total(same & (down < across), 1.0, 0)
        other_opens = other_rank == 2.0 * jnp.floor(other_rank * 0.5)
        own_part, other_part = part_of(key), part_of(other)
        group = jnp.floor(rank * 0.5)
        opens = rank == 2.0 * group
        group += total((other < key) & (own_part == other_part) & other_opens, 1.0, 1)
        word = jnp.where(opens, left * scale[0] + key - own_part * cut, left * scale[1])
        for part in range(parts):
            counted = (own_part == float(part)) & (key < dead)
            words = empty + total(counted & (group == places), word, 0)
            words = jnp.where(places == width - 1.0, total(counted & opens, 1.0, 0), words)
            line = parts * stop + part
            words_ref[line : line + 1, :] = words.astype(jnp.int32)


def products_kernel(sizes, n_rights, layout, opens, closes, words_ref, *refs):
    n_sources = sizes.n_col if opens else 1
    sources, refs = refs[:n_sources], refs[n_sources:]
    right_refs, refs = refs[:n_rights], refs[n_rights:]
    start_ref = None
    if not opens:
        start_ref, refs = refs[0], refs[1:]
    out_ref, refs = refs[0], refs[1:]
    left_ref = sources[0]
    edge = sizes.edge
    if opens:
        left_ref, refs = refs[0], refs[1:]
        rows = sizes.n_left * edge
        for j, source in enumerate(sources):
            left_ref[j * rows : (j + 1) * rows, :] = source[...]
        left_ref[len(sources) * rows :, :] = jnp.zeros((edge, edge), left_ref.dtype)
    ids_ref, col_ref, copy_sem = refs[:3]
    total_ref = refs[3] if closes else out_ref
    for which, ref in enumerate(right_refs):
        ids_ref[which : which + 1, :] = ids_of(ref).astype(jnp.int32)
    copy = pltpu.make_async_copy(ids_ref, col_ref, copy_sem)
    copy.start()
    total_ref[...] = jnp.zeros_like(total_ref) if opens else start_ref[...]
    copy.wait()

    core, col = lax.rem(lax.axis_index("row"), 2), lax.axis_index("col")

    def block(ref, slot, head):
        return ref[pl.ds(pl.multiple_of(slot * edge + head, HEAD_STEP), edge), :]

    for array, head, part, ahead in layout:
        stop = jnp.where(
            core == 0,
            -1 if ahead[0] is None else ahead[0] - col,
            -1 if ahead[1] is None else ahead[1] - col,
        )
        used = (stop >= 0) & (stop < sizes.n_stops)
        line = jnp.clip(stop, 0, sizes.n_stops - 1) * sizes.parts + part
        count = jnp.where(used, words_ref[line, sizes.width - 1], 0)

        def groups(first, size, array=array, head=head, part=part, line=line):
            for member in range(size):
                word = words_ref[line, first + member]
                row = word & ((1 << sizes.row_bits) - 1)
                slot = (word & ((1 << sizes.key_bits) - 1)) >> sizes.row_bits
                word = word >> sizes.key_bits
                lefts = word & ((1 << sizes.left_bits) - 1), word >> sizes.left_bits
                target = row * CCOLS + col_ref[array, slot + sizes.cuts[part]]
                right = block(right_refs[array], slot, head)
                total_ref[target] += jnp.dot(
                    jnp.concatenate([block(left_ref, left, 0) for left in lefts], axis=1),
                    jnp.concatenate([right, right], axis=0),
                    preferred_element_type=jnp.float32,
                )

        steps = (count + UNROLL // 2 - 1) // UNROLL

        @pl.loop(0, steps)
        def _(step, groups=groups):
            groups(step * UNROLL, UNROLL)

        @pl.when(count > steps * UNROLL)
        def _(steps=steps, groups=groups):
            groups(steps * UNROLL, UNROLL // 2)

    if closes:
        for target in range(total_ref.shape[0]):
            row, col = divmod(target, CCOLS)
            out_ref[row * edge : (row + 1) * edge, col * edge : (col + 1) * edge] = total_ref[
                target
            ].astype(out_ref.dtype)


def per_device(a_blocks, a_rows, b_blocks, b_cols, pair_list, pair_count, row_order):
    n_row, n_col = lax.axis_size("row"), lax.axis_size("col")
    n_stops, n_pairs = pair_list.shape[2], pair_list.shape[4]
    sizes = Sizes(
        n_stops,
        n_pairs,
        a_blocks.shape[2],
        b_blocks.shape[2],
        row_order.shape[1],
        n_col,
        a_blocks.shape[3],
    )
    row = lax.axis_index("row")
    edge, sums = sizes.edge, (sizes.n_rows * CCOLS, sizes.edge, sizes.edge)
    reach = n_col + n_stops - 2
    chips = (reach + 1) // 2
    evens, odds = range(2, chips + 1, 2), range(1, chips + 1, 2)
    parts = range(PARTS)

    def from_ahead(block, axis, distance):
        size = lax.axis_size(axis)
        return lax.ppermute(block, axis, [((i + distance) % size, i) for i in range(size)])

    def swap(bit, lower, upper, skip=0):
        mine = lower if lower is upper else jnp.where(row // bit % 2 == 1, upper, lower)
        mine = mine[skip:]
        return lax.ppermute(mine, "row", [(i ^ bit, i) for i in range(n_row)])

    def both(distance):
        return (distance, distance)

    def swapped(j):
        ahead = 2 * j + 1, 2 * j - 1
        return tuple(d if 1 <= d <= reach else None for d in ahead)

    own = pack(sizes, b_blocks, b_cols)
    even = {j: [from_ahead(part, "row", 2 * j) for part in own] for j in range(2, chips + 2, 2)}
    left_ids, left_own = a_rows.reshape(1, -1), a_blocks.reshape(-1, edge)
    left_ids = [left_ids] + [from_ahead(left_ids, "col", j) for j in range(1, n_col)]
    lefts = [left_own] + [from_ahead(left_own, "col", j) for j in range(1, n_col)]
    words = kernel_call(
        functools.partial(prepare_kernel, sizes),
        jax.ShapeDtypeStruct((PARTS * n_stops, sizes.width), jnp.int32),
        [pair_count.reshape(1, -1), row_order, pair_list.reshape(2 * n_stops, n_pairs).T]
        + left_ids,
        flops=1 << 34,
    )

    def wait(part, *others):
        arrived, others = lax.optimization_barrier(([even[j][part] for j in even], others))
        for j, block in zip(even, arrived):
            even[j][part] = block
        return others

    def pass_on(part):
        sets = {0: own, **even}
        return {j: swap(2, sets[j + 1][part], sets[j - 1][part]) for j in odds}

    def add(total, pieces, closes=False):
        rights = list({id(piece[0]): piece[0] for piece in pieces}.values())
        places = {id(block): place for place, block in enumerate(rights)}
        layout = tuple((places[id(piece[0])], *piece[1:]) for piece in pieces)
        if closes:
            out_shape = jax.ShapeDtypeStruct((sizes.n_rows * edge, CCOLS * edge), jnp.bfloat16)
        else:
            out_shape = jax.ShapeDtypeStruct(sums, jnp.float32)
        if total is None:
            left_shape = ((sizes.zero_slot + 1) * edge, edge)
            out_shape = [out_shape, jax.ShapeDtypeStruct(left_shape, b_blocks.dtype)]
        lines = round_up(len(rights), 8)
        return kernel_call(
            functools.partial(
                products_kernel, sizes, len(rights), layout, total is None, closes
            ),
            out_shape,
            (lefts if total is None else [left_all])
            + rights
            + ([] if total is None else [total]),
            [words],
            [
                pltpu.VMEM((lines, 128), jnp.int32),
                pltpu.SMEM((lines, 128), jnp.int32),
                pltpu.SemaphoreType.DMA,
            ]
            + ([pltpu.VMEM(sums, jnp.float32)] if closes else []),
        )

    def pieces_of(j, part, block):
        skip = HEAD_STEP if j in evens else 0
        theirs = swap(1, block, block, skip)
        return [
            (block, HEAD, part, both(2 * j)),
            (theirs, HEAD - skip, part, swapped(j)),
        ]

    odd = {}
    (words,) = wait(0, words)
    odd[0] = pass_on(0)
    own_first, own_last = pieces_of(0, 0, own[0]), pieces_of(0, 1, own[1])
    pieces = own_first + own_last[:1]
    pieces += [piece for j in evens for piece in pieces_of(j, 0, even[j][0])]
    total, left_all = add(None, pieces)
    odd[0], total = wait(1, odd[0], total)
    odd[1] = pass_on(1)
    pieces = own_last[1:]
    pieces += [piece for j in odds for piece in pieces_of(j, 0, odd[0][j])]
    pieces += [piece for j in evens for piece in pieces_of(j, 1, even[j][1])]
    total = add(total, pieces)
    odd[1], total = lax.optimization_barrier((odd[1], total))
    pieces = [piece for j in odds for piece in pieces_of(j, 1, odd[1][j])]
    return add(total, pieces, closes=True)


def solution(mesh):
    placed = (
        P("row", "col", None, None, None),
        P("row", "col", None),
        P("row", "col", None, None, None),
        P("row", "col", None),
        P("row", "col", None, None, None),
        P("row", "col", None),
        P("row", None),
    )
    return jax.shard_map(
        per_device, mesh=mesh, in_specs=placed, out_specs=P("row", "col"), check_vma=False
    )
```

```python
import functools

import jax
import jax.numpy as jnp
from jax import lax
from jax.experimental import pallas as pl
from jax.experimental.pallas import tpu as pltpu
from jax.sharding import PartitionSpec as P

CCOLS = 8
SHARES = (10, 21, 32)
PARTS = len(SHARES)
UNROLL = 16
HEADS = (32, 32, 48)
HEAD_STEP = 16
VMEM_BYTES = 40 << 20
VMEM = pl.BlockSpec(memory_space=pltpu.VMEM)


def round_up(value, step):
    return value + -value % step


class Sizes:
    def __init__(self, n_stops, n_pairs, n_left, n_right, n_rows, n_col, edge):
        self.n_stops, self.n_pairs, self.n_rows, self.n_col = n_stops, n_pairs, n_rows, n_col
        self.n_left, self.n_right, self.edge = n_left, n_right, edge
        self.parts = PARTS
        self.cuts = (0, *(n_right * share // SHARES[-1] for share in SHARES))
        self.per_part = max(high - low for low, high in zip(self.cuts, self.cuts[1:]))
        self.zero_slot = n_col * n_left
        self.row_bits = (n_rows - 1).bit_length()
        self.key_bits = self.row_bits + (self.per_part - 1).bit_length()
        self.left_bits = self.zero_slot.bit_length()
        most = (n_pairs + self.per_part * n_rows) // 2
        self.width = round_up(round_up(most, UNROLL) + 1, 128)


def kernel_call(
    kernel,
    out_shape,
    operands,
    scalars=(),
    scratch=(),
    specs=None,
    flops=128,
):
    return pl.pallas_call(
        kernel,
        out_shape=out_shape,
        grid_spec=pltpu.PrefetchScalarGridSpec(
            num_scalar_prefetch=len(scalars),
            in_specs=specs or [VMEM] * len(operands),
            out_specs=jax.tree.map(lambda _: VMEM, out_shape),
            scratch_shapes=list(scratch),
        ),
        compiler_params=pltpu.CompilerParams(vmem_limit_bytes=VMEM_BYTES),
        cost_estimate=pl.CostEstimate(flops=flops, bytes_accessed=128, transcendentals=0),
    )(*scalars, *operands)


def pack_kernel(cuts, blocks_ref, ids_ref, *refs):
    part_refs, head_ref, sems = refs[:-2], refs[-2], refs[-1]
    edge = blocks_ref.shape[1]
    copies = []
    for part, ref in enumerate(part_refs):
        low, count = cuts[part] * edge, (cuts[part + 1] - cuts[part]) * edge
        source, target = blocks_ref.at[pl.ds(low, count)], ref.at[pl.ds(HEADS[part], count)]
        copies.append(pltpu.make_async_copy(source, target, sems.at[part]))
    for copy in copies:
        copy.start()
    head_ref[...] = jnp.zeros_like(head_ref)
    head_ref[0:1, : ids_ref.shape[1]] = ids_ref[...].astype(jnp.float32)
    for head, ref in zip(HEADS, part_refs):
        for row in range(0, head, HEAD_STEP):
            ref[row : row + HEAD_STEP, :] = head_ref[...].astype(ref.dtype)
    for copy in copies:
        copy.wait()


def pack(sizes, blocks, ids):
    edge = sizes.edge
    counts = [high - low for low, high in zip(sizes.cuts, sizes.cuts[1:])]
    shapes = [(head + count * edge, edge) for head, count in zip(HEADS, counts)]
    return kernel_call(
        functools.partial(pack_kernel, sizes.cuts),
        [jax.ShapeDtypeStruct(shape, blocks.dtype) for shape in shapes],
        [blocks.reshape(-1, edge), ids.reshape(1, -1)],
        scratch=[pltpu.VMEM((HEAD_STEP, edge), jnp.float32), pltpu.SemaphoreType.DMA((PARTS,))],
        specs=[pl.BlockSpec(memory_space=pl.ANY), VMEM],
    )


def ids_of(ref):
    return ref[:HEAD_STEP, :].astype(jnp.float32)[0:1, :]


def prepare_kernel(sizes, count_ref, order_ref, pairs_ref, *refs):
    words_ref = refs[-1]
    id_sets = [ref[...] for ref in refs[:-1]]
    n_col, n_rows, parts = sizes.n_col, sizes.n_rows, sizes.parts
    n_pairs, width = sizes.n_pairs, sizes.width

    def total(mask, value, axis):
        return jnp.sum(jnp.where(mask, value, 0.0), axis=axis, keepdims=True)

    here = lax.axis_index("row")
    lane = lax.broadcasted_iota(jnp.int32, (n_pairs, 128), 1)
    slot = lane[:, : sizes.n_left]
    down = lax.broadcasted_iota(jnp.int32, (n_pairs, 1), 0)
    across = lax.broadcasted_iota(jnp.int32, (1, n_pairs), 1)
    places = lax.broadcasted_iota(jnp.int32, (1, width), 1).astype(jnp.float32)
    dead = float(sizes.n_right * n_rows)
    lefts, keys = [], []
    key_matrix = jnp.zeros((n_pairs, 128), jnp.float32)
    for stop in range(sizes.n_stops):
        ahead = lax.rem(here + stop, n_col)
        ids = id_sets[0]
        for j in range(1, n_col):
            ids = jnp.where(ahead == j, id_sets[j], ids)
        left_row = jnp.zeros(ids.shape, jnp.float32)
        for i in range(n_rows):
            left_row = jnp.where(ids == i, order_ref[:, i : i + 1].astype(jnp.float32), left_row)
        left = pairs_ref[:, 2 * stop : 2 * stop + 1]
        right = pairs_ref[:, 2 * stop + 1 : 2 * stop + 2]
        key = right.astype(jnp.float32) * n_rows + total(slot == left, left_row, 1)
        key = jnp.where(down < count_ref[:, stop : stop + 1], key, dead)
        lefts.append((left + ahead * sizes.n_left - sizes.zero_slot).astype(jnp.float32))
        keys.append(key)
        key_matrix = jnp.where(lane == stop, key, key_matrix)
    key_rows = key_matrix.T
    cuts = [float(cut * n_rows) for cut in sizes.cuts]

    def part_of(key):
        return sum(jnp.where(key >= cut, 1.0, 0.0) for cut in cuts[1:-1])

    def start_of(key):
        low = jnp.zeros_like(key)
        for cut in cuts[1:-1]:
            low = jnp.where(key >= cut, cut, low)
        return low

    scale = [float(1 << sizes.key_bits), float(1 << (sizes.key_bits + sizes.left_bits))]
    empty = sizes.zero_slot * (scale[0] + scale[1])
    for stop in range(sizes.n_stops):
        left, key, other = lefts[stop], keys[stop], key_rows[stop : stop + 1, :]
        same = key == other
        rank = total(same & (across < down), 1.0, 1)
        other_rank = total(same & (down < across), 1.0, 0)
        other_opens = other_rank == 2.0 * jnp.floor(other_rank * 0.5)
        own_part, other_part = part_of(key), part_of(other)
        group = jnp.floor(rank * 0.5)
        opens = rank == 2.0 * group
        group += total((other < key) & (own_part == other_part) & other_opens, 1.0, 1)
        word = jnp.where(opens, left * scale[0] + key - start_of(key), left * scale[1])
        for part in range(parts):
            counted = (own_part == float(part)) & (key < dead)
            words = empty + total(counted & (group == places), word, 0)
            words = jnp.where(places == width - 1.0, total(counted & opens, 1.0, 0), words)
            line = parts * stop + part
            words_ref[line : line + 1, :] = words.astype(jnp.int32)


def products_kernel(sizes, n_rights, layout, opens, closes, words_ref, *refs):
    n_sources = sizes.n_col if opens else 1
    sources, refs = refs[:n_sources], refs[n_sources:]
    right_refs, refs = refs[:n_rights], refs[n_rights:]
    start_ref = None
    if not opens:
        start_ref, refs = refs[0], refs[1:]
    out_ref, refs = refs[0], refs[1:]
    left_ref = sources[0]
    edge = sizes.edge
    if opens:
        left_ref, refs = refs[0], refs[1:]
        rows = sizes.n_left * edge
        for j, source in enumerate(sources):
            left_ref[j * rows : (j + 1) * rows, :] = source[...]
        left_ref[len(sources) * rows :, :] = jnp.zeros((edge, edge), left_ref.dtype)
    ids_ref, col_ref, copy_sem = refs[:3]
    total_ref = refs[3] if closes else out_ref
    for which, ref in enumerate(right_refs):
        ids_ref[which : which + 1, :] = ids_of(ref).astype(jnp.int32)
    copy = pltpu.make_async_copy(ids_ref, col_ref, copy_sem)
    copy.start()
    total_ref[...] = jnp.zeros_like(total_ref) if opens else start_ref[...]
    copy.wait()

    core, col = lax.rem(lax.axis_index("row"), 2), lax.axis_index("col")

    def block(ref, slot, head):
        return ref[pl.ds(pl.multiple_of(slot * edge + head, HEAD_STEP), edge), :]

    for array, head, part, ahead in layout:
        stop = jnp.where(
            core == 0,
            -1 if ahead[0] is None else ahead[0] - col,
            -1 if ahead[1] is None else ahead[1] - col,
        )
        used = (stop >= 0) & (stop < sizes.n_stops)
        line = jnp.clip(stop, 0, sizes.n_stops - 1) * sizes.parts + part
        count = jnp.where(used, words_ref[line, sizes.width - 1], 0)

        def groups(first, size, array=array, head=head, part=part, line=line):
            for member in range(size):
                word = words_ref[line, first + member]
                row = word & ((1 << sizes.row_bits) - 1)
                slot = (word & ((1 << sizes.key_bits) - 1)) >> sizes.row_bits
                word = word >> sizes.key_bits
                lefts = word & ((1 << sizes.left_bits) - 1), word >> sizes.left_bits
                target = row * CCOLS + col_ref[array, slot + sizes.cuts[part]]
                right = block(right_refs[array], slot, head)
                total_ref[target] += jnp.dot(
                    jnp.concatenate([block(left_ref, left, 0) for left in lefts], axis=1),
                    jnp.concatenate([right, right], axis=0),
                    preferred_element_type=jnp.float32,
                )

        steps = (count + UNROLL // 2 - 1) // UNROLL

        @pl.loop(0, steps)
        def _(step, groups=groups):
            groups(step * UNROLL, UNROLL)

        @pl.when(count > steps * UNROLL)
        def _(steps=steps, groups=groups):
            groups(steps * UNROLL, UNROLL // 2)

    if closes:
        for target in range(total_ref.shape[0]):
            row, col = divmod(target, CCOLS)
            out_ref[row * edge : (row + 1) * edge, col * edge : (col + 1) * edge] = total_ref[
                target
            ].astype(out_ref.dtype)


def per_device(a_blocks, a_rows, b_blocks, b_cols, pair_list, pair_count, row_order):
    n_row, n_col = lax.axis_size("row"), lax.axis_size("col")
    n_stops, n_pairs = pair_list.shape[2], pair_list.shape[4]
    sizes = Sizes(
        n_stops,
        n_pairs,
        a_blocks.shape[2],
        b_blocks.shape[2],
        row_order.shape[1],
        n_col,
        a_blocks.shape[3],
    )
    row = lax.axis_index("row")
    edge, sums = sizes.edge, (sizes.n_rows * CCOLS, sizes.edge, sizes.edge)
    reach = n_col + n_stops - 2
    chips = (reach + 1) // 2
    evens, odds = range(2, chips + 1, 2), range(1, chips + 1, 2)
    parts = range(PARTS)

    def from_ahead(block, axis, distance):
        size = lax.axis_size(axis)
        return lax.ppermute(block, axis, [((i + distance) % size, i) for i in range(size)])

    def swap(bit, lower, upper, skip=0):
        mine = lower if lower is upper else jnp.where(row // bit % 2 == 1, upper, lower)
        mine = mine[skip:]
        return lax.ppermute(mine, "row", [(i ^ bit, i) for i in range(n_row)])

    def both(distance):
        return (distance, distance)

    def swapped(j):
        ahead = 2 * j + 1, 2 * j - 1
        return tuple(d if 1 <= d <= reach else None for d in ahead)

    own = pack(sizes, b_blocks, b_cols)
    even = {j: [from_ahead(part, "row", 2 * j) for part in own] for j in range(2, chips + 2, 2)}
    left_ids, left_own = a_rows.reshape(1, -1), a_blocks.reshape(-1, edge)
    left_ids = [left_ids] + [from_ahead(left_ids, "col", j) for j in range(1, n_col)]
    lefts = [left_own] + [from_ahead(left_own, "col", j) for j in range(1, n_col)]
    words = kernel_call(
        functools.partial(prepare_kernel, sizes),
        jax.ShapeDtypeStruct((PARTS * n_stops, sizes.width), jnp.int32),
        [pair_count.reshape(1, -1), row_order, pair_list.reshape(2 * n_stops, n_pairs).T]
        + left_ids,
        flops=1 << 34,
    )

    def wait(part, *others):
        arrived, others = lax.optimization_barrier(([even[j][part] for j in even], others))
        for j, block in zip(even, arrived):
            even[j][part] = block
        return others

    def pass_on(part):
        sets = {0: own, **even}
        return {j: swap(2, sets[j + 1][part], sets[j - 1][part]) for j in odds}

    def add(total, pieces, closes=False):
        rights = list({id(piece[0]): piece[0] for piece in pieces}.values())
        places = {id(block): place for place, block in enumerate(rights)}
        layout = tuple((places[id(piece[0])], *piece[1:]) for piece in pieces)
        if closes:
            out_shape = jax.ShapeDtypeStruct((sizes.n_rows * edge, CCOLS * edge), jnp.bfloat16)
        else:
            out_shape = jax.ShapeDtypeStruct(sums, jnp.float32)
        if total is None:
            left_shape = ((sizes.zero_slot + 1) * edge, edge)
            out_shape = [out_shape, jax.ShapeDtypeStruct(left_shape, b_blocks.dtype)]
        lines = round_up(len(rights), 8)
        return kernel_call(
            functools.partial(
                products_kernel, sizes, len(rights), layout, total is None, closes
            ),
            out_shape,
            (lefts if total is None else [left_all])
            + rights
            + ([] if total is None else [total]),
            [words],
            [
                pltpu.VMEM((lines, 128), jnp.int32),
                pltpu.SMEM((lines, 128), jnp.int32),
                pltpu.SemaphoreType.DMA,
            ]
            + ([pltpu.VMEM(sums, jnp.float32)] if closes else []),
        )

    def pieces_of(j, part, block):
        skip = HEAD_STEP if j in evens else 0
        theirs = swap(1, block, block, skip)
        return [
            (block, HEADS[part], part, both(2 * j)),
            (theirs, HEADS[part] - skip, part, swapped(j)),
        ]

    def odd_pieces(part):
        return [piece for j in odds for piece in pieces_of(j, part, odd[part][j])]

    def even_pieces(part):
        return [piece for j in evens for piece in pieces_of(j, part, even[j][part])]

    odd = {}
    wait(0)
    odd[0] = pass_on(0)
    own_pieces = [pieces_of(0, part, own[part]) for part in parts]
    pieces = [mine for mine, _ in own_pieces] + [own_pieces[0][1]]
    total, left_all = add(None, pieces + even_pieces(0))
    for part in parts[1:]:
        odd[part - 1], total = wait(part, odd[part - 1], total)
        odd[part] = pass_on(part)
        pieces = [own_pieces[part][1]] + odd_pieces(part - 1) + even_pieces(part)
        total = add(total, pieces)
    odd[PARTS - 1], total = lax.optimization_barrier((odd[PARTS - 1], total))
    return add(total, odd_pieces(PARTS - 1), closes=True)


def solution(mesh):
    placed = (
        P("row", "col", None, None, None),
        P("row", "col", None),
        P("row", "col", None, None, None),
        P("row", "col", None),
        P("row", "col", None, None, None),
        P("row", "col", None),
        P("row", None),
    )
    return jax.shard_map(
        per_device, mesh=mesh, in_specs=placed, out_specs=P("row", "col"), check_vma=False
    )
```

```python
import functools

import jax
import jax.numpy as jnp
from jax import lax
from jax.experimental import pallas as pl
from jax.experimental.pallas import tpu as pltpu
from jax.sharding import PartitionSpec as P

CCOLS = 8
PARTS = 2
FIRST_PART = 15, 32
UNROLL = 32
HEAD = 32
HEAD_STEP = 16
VMEM_BYTES = 40 << 20
VMEM = pl.BlockSpec(memory_space=pltpu.VMEM)


def round_up(value, step):
    return value + -value % step


class Sizes:
    def __init__(self, n_stops, n_pairs, n_left, n_right, n_rows, n_col, edge):
        self.n_stops, self.n_pairs, self.n_rows, self.n_col = n_stops, n_pairs, n_rows, n_col
        self.n_left, self.n_right, self.edge = n_left, n_right, edge
        self.parts = PARTS
        first = n_right * FIRST_PART[0] // FIRST_PART[1]
        self.cuts = (0, first, n_right)
        self.per_part = max(first, n_right - first)
        self.zero_slot = n_col * n_left
        self.row_bits = (n_rows - 1).bit_length()
        self.key_bits = self.row_bits + (self.per_part - 1).bit_length()
        self.left_bits = self.zero_slot.bit_length()
        most = (n_pairs + self.per_part * n_rows) // 2
        self.width = round_up(round_up(most, UNROLL) + 1, 128)


def kernel_call(
    kernel,
    out_shape,
    operands,
    scalars=(),
    scratch=(),
    specs=None,
    flops=128,
):
    return pl.pallas_call(
        kernel,
        out_shape=out_shape,
        grid_spec=pltpu.PrefetchScalarGridSpec(
            num_scalar_prefetch=len(scalars),
            in_specs=specs or [VMEM] * len(operands),
            out_specs=jax.tree.map(lambda _: VMEM, out_shape),
            scratch_shapes=list(scratch),
        ),
        compiler_params=pltpu.CompilerParams(vmem_limit_bytes=VMEM_BYTES),
        cost_estimate=pl.CostEstimate(flops=flops, bytes_accessed=128, transcendentals=0),
    )(*scalars, *operands)


def pack_kernel(cuts, blocks_ref, ids_ref, *refs):
    part_refs, head_ref, sems = refs[:-2], refs[-2], refs[-1]
    edge = blocks_ref.shape[1]
    copies = []
    for part, ref in enumerate(part_refs):
        low, count = cuts[part] * edge, (cuts[part + 1] - cuts[part]) * edge
        source, target = blocks_ref.at[pl.ds(low, count)], ref.at[pl.ds(HEAD, count)]
        copies.append(pltpu.make_async_copy(source, target, sems.at[part]))
    for copy in copies:
        copy.start()
    head_ref[...] = jnp.zeros_like(head_ref)
    head_ref[0:1, : ids_ref.shape[1]] = ids_ref[...].astype(jnp.float32)
    for ref in part_refs:
        for row in range(0, HEAD, HEAD_STEP):
            ref[row : row + HEAD_STEP, :] = head_ref[...].astype(ref.dtype)
    for copy in copies:
        copy.wait()


def pack(sizes, blocks, ids):
    edge = sizes.edge
    counts = [high - low for low, high in zip(sizes.cuts, sizes.cuts[1:])]
    shapes = [(HEAD + count * edge, edge) for count in counts]
    return kernel_call(
        functools.partial(pack_kernel, sizes.cuts),
        [jax.ShapeDtypeStruct(shape, blocks.dtype) for shape in shapes],
        [blocks.reshape(-1, edge), ids.reshape(1, -1)],
        scratch=[pltpu.VMEM((HEAD_STEP, edge), jnp.float32), pltpu.SemaphoreType.DMA((PARTS,))],
        specs=[pl.BlockSpec(memory_space=pl.ANY), VMEM],
    )


def ids_of(ref):
    return ref[:HEAD_STEP, :].astype(jnp.float32)[0:1, :]


def prepare_kernel(sizes, count_ref, order_ref, pairs_ref, *refs):
    words_ref = refs[-1]
    id_sets = [ref[...] for ref in refs[:-1]]
    n_col, n_rows, parts = sizes.n_col, sizes.n_rows, sizes.parts
    n_pairs, width = sizes.n_pairs, sizes.width

    def total(mask, value, axis):
        return jnp.sum(jnp.where(mask, value, 0.0), axis=axis, keepdims=True)

    here = lax.axis_index("row")
    lane = lax.broadcasted_iota(jnp.int32, (n_pairs, 128), 1)
    slot = lane[:, : sizes.n_left]
    down = lax.broadcasted_iota(jnp.int32, (n_pairs, 1), 0)
    across = lax.broadcasted_iota(jnp.int32, (1, n_pairs), 1)
    places = lax.broadcasted_iota(jnp.int32, (1, width), 1).astype(jnp.float32)
    dead = float(sizes.n_right * n_rows)
    lefts, keys = [], []
    key_matrix = jnp.zeros((n_pairs, 128), jnp.float32)
    for stop in range(sizes.n_stops):
        ahead = lax.rem(here + stop, n_col)
        ids = id_sets[0]
        for j in range(1, n_col):
            ids = jnp.where(ahead == j, id_sets[j], ids)
        left_row = jnp.zeros(ids.shape, jnp.float32)
        for i in range(n_rows):
            left_row = jnp.where(ids == i, order_ref[:, i : i + 1].astype(jnp.float32), left_row)
        left = pairs_ref[:, 2 * stop : 2 * stop + 1]
        right = pairs_ref[:, 2 * stop + 1 : 2 * stop + 2]
        key = right.astype(jnp.float32) * n_rows + total(slot == left, left_row, 1)
        key = jnp.where(down < count_ref[:, stop : stop + 1], key, dead)
        lefts.append((left + ahead * sizes.n_left - sizes.zero_slot).astype(jnp.float32))
        keys.append(key)
        key_matrix = jnp.where(lane == stop, key, key_matrix)
    key_rows = key_matrix.T
    cut = float(sizes.cuts[1] * n_rows)

    def part_of(key):
        return jnp.where(key >= cut, 1.0, 0.0)

    scale = [float(1 << sizes.key_bits), float(1 << (sizes.key_bits + sizes.left_bits))]
    empty = sizes.zero_slot * (scale[0] + scale[1])
    for stop in range(sizes.n_stops):
        left, key, other = lefts[stop], keys[stop], key_rows[stop : stop + 1, :]
        same = key == other
        rank = total(same & (across < down), 1.0, 1)
        other_rank = total(same & (down < across), 1.0, 0)
        other_opens = other_rank == 2.0 * jnp.floor(other_rank * 0.5)
        own_part, other_part = part_of(key), part_of(other)
        group = jnp.floor(rank * 0.5)
        opens = rank == 2.0 * group
        group += total((other < key) & (own_part == other_part) & other_opens, 1.0, 1)
        word = jnp.where(opens, left * scale[0] + key - own_part * cut, left * scale[1])
        for part in range(parts):
            counted = (own_part == float(part)) & (key < dead)
            words = empty + total(counted & (group == places), word, 0)
            words = jnp.where(places == width - 1.0, total(counted & opens, 1.0, 0), words)
            line = parts * stop + part
            words_ref[line : line + 1, :] = words.astype(jnp.int32)


def products_kernel(sizes, n_rights, layout, opens, closes, words_ref, *refs):
    n_sources = sizes.n_col if opens else 1
    sources, refs = refs[:n_sources], refs[n_sources:]
    right_refs, refs = refs[:n_rights], refs[n_rights:]
    start_ref = None
    if not opens:
        start_ref, refs = refs[0], refs[1:]
    out_ref, refs = refs[0], refs[1:]
    left_ref = sources[0]
    edge = sizes.edge
    if opens:
        left_ref, refs = refs[0], refs[1:]
        rows = sizes.n_left * edge
        for j, source in enumerate(sources):
            left_ref[j * rows : (j + 1) * rows, :] = source[...]
        left_ref[len(sources) * rows :, :] = jnp.zeros((edge, edge), left_ref.dtype)
    ids_ref, col_ref, copy_sem = refs[:3]
    total_ref = refs[3] if closes else out_ref
    for which, ref in enumerate(right_refs):
        ids_ref[which : which + 1, :] = ids_of(ref).astype(jnp.int32)
    copy = pltpu.make_async_copy(ids_ref, col_ref, copy_sem)
    copy.start()
    total_ref[...] = jnp.zeros_like(total_ref) if opens else start_ref[...]
    copy.wait()

    core, col = lax.rem(lax.axis_index("row"), 2), lax.axis_index("col")

    def block(ref, slot, head):
        return ref[pl.ds(pl.multiple_of(slot * edge + head, HEAD_STEP), edge), :]

    for array, head, part, ahead in layout:
        stop = jnp.where(
            core == 0,
            -1 if ahead[0] is None else ahead[0] - col,
            -1 if ahead[1] is None else ahead[1] - col,
        )
        used = (stop >= 0) & (stop < sizes.n_stops)
        line = jnp.clip(stop, 0, sizes.n_stops - 1) * sizes.parts + part
        count = jnp.where(used, words_ref[line, sizes.width - 1], 0)

        def groups(first, size, array=array, head=head, part=part, line=line):
            for member in range(size):
                word = words_ref[line, first + member]
                row = word & ((1 << sizes.row_bits) - 1)
                slot = (word & ((1 << sizes.key_bits) - 1)) >> sizes.row_bits
                word = word >> sizes.key_bits
                lefts = word & ((1 << sizes.left_bits) - 1), word >> sizes.left_bits
                target = row * CCOLS + col_ref[array, slot + sizes.cuts[part]]
                right = block(right_refs[array], slot, head)
                total_ref[target] += jnp.dot(
                    jnp.concatenate([block(left_ref, left, 0) for left in lefts], axis=1),
                    jnp.concatenate([right, right], axis=0),
                    preferred_element_type=jnp.float32,
                )

        steps = (count + UNROLL // 2 - 1) // UNROLL

        @pl.loop(0, steps)
        def _(step, groups=groups):
            groups(step * UNROLL, UNROLL)

        @pl.when(count > steps * UNROLL)
        def _(steps=steps, groups=groups):
            groups(steps * UNROLL, UNROLL // 2)

    if closes:
        for target in range(total_ref.shape[0]):
            row, col = divmod(target, CCOLS)
            out_ref[row * edge : (row + 1) * edge, col * edge : (col + 1) * edge] = total_ref[
                target
            ].astype(out_ref.dtype)


def per_device(a_blocks, a_rows, b_blocks, b_cols, pair_list, pair_count, row_order):
    n_row, n_col = lax.axis_size("row"), lax.axis_size("col")
    n_stops, n_pairs = pair_list.shape[2], pair_list.shape[4]
    sizes = Sizes(
        n_stops,
        n_pairs,
        a_blocks.shape[2],
        b_blocks.shape[2],
        row_order.shape[1],
        n_col,
        a_blocks.shape[3],
    )
    row = lax.axis_index("row")
    edge, sums = sizes.edge, (sizes.n_rows * CCOLS, sizes.edge, sizes.edge)
    reach = n_col + n_stops - 2
    chips = (reach + 1) // 2
    evens, odds = range(2, chips + 1, 2), range(1, chips + 1, 2)
    parts = range(PARTS)

    def from_ahead(block, axis, distance):
        size = lax.axis_size(axis)
        return lax.ppermute(block, axis, [((i + distance) % size, i) for i in range(size)])

    def swap(bit, lower, upper, skip=0):
        mine = lower if lower is upper else jnp.where(row // bit % 2 == 1, upper, lower)
        mine = mine[skip:]
        return lax.ppermute(mine, "row", [(i ^ bit, i) for i in range(n_row)])

    def both(distance):
        return (distance, distance)

    def swapped(j):
        ahead = 2 * j + 1, 2 * j - 1
        return tuple(d if 1 <= d <= reach else None for d in ahead)

    own = pack(sizes, b_blocks, b_cols)
    even = {j: [from_ahead(part, "row", 2 * j) for part in own] for j in range(2, chips + 2, 2)}
    left_ids, left_own = a_rows.reshape(1, -1), a_blocks.reshape(-1, edge)
    left_ids = [left_ids] + [from_ahead(left_ids, "col", j) for j in range(1, n_col)]
    lefts = [left_own] + [from_ahead(left_own, "col", j) for j in range(1, n_col)]
    words = kernel_call(
        functools.partial(prepare_kernel, sizes),
        jax.ShapeDtypeStruct((PARTS * n_stops, sizes.width), jnp.int32),
        [pair_count.reshape(1, -1), row_order, pair_list.reshape(2 * n_stops, n_pairs).T]
        + left_ids,
        flops=1 << 34,
    )

    def wait(part, *others):
        arrived, others = lax.optimization_barrier(([even[j][part] for j in even], others))
        for j, block in zip(even, arrived):
            even[j][part] = block
        return others

    def pass_on(part):
        sets = {0: own, **even}
        return {j: swap(2, sets[j + 1][part], sets[j - 1][part]) for j in odds}

    def add(total, pieces, closes=False):
        rights = list({id(piece[0]): piece[0] for piece in pieces}.values())
        places = {id(block): place for place, block in enumerate(rights)}
        layout = tuple((places[id(piece[0])], *piece[1:]) for piece in pieces)
        if closes:
            out_shape = jax.ShapeDtypeStruct((sizes.n_rows * edge, CCOLS * edge), jnp.bfloat16)
        else:
            out_shape = jax.ShapeDtypeStruct(sums, jnp.float32)
        if total is None:
            left_shape = ((sizes.zero_slot + 1) * edge, edge)
            out_shape = [out_shape, jax.ShapeDtypeStruct(left_shape, b_blocks.dtype)]
        lines = round_up(len(rights), 8)
        return kernel_call(
            functools.partial(
                products_kernel, sizes, len(rights), layout, total is None, closes
            ),
            out_shape,
            (lefts if total is None else [left_all])
            + rights
            + ([] if total is None else [total]),
            [words],
            [
                pltpu.VMEM((lines, 128), jnp.int32),
                pltpu.SMEM((lines, 128), jnp.int32),
                pltpu.SemaphoreType.DMA,
            ]
            + ([pltpu.VMEM(sums, jnp.float32)] if closes else []),
        )

    def pieces_of(j, part, block):
        skip = HEAD_STEP if j in evens else 0
        theirs = swap(1, block, block, skip)
        return [
            (block, HEAD, part, both(2 * j)),
            (theirs, HEAD - skip, part, swapped(j)),
        ]

    odd = {}
    (words,) = wait(0, words)
    odd[0] = pass_on(0)
    own_first, own_last = pieces_of(0, 0, own[0]), pieces_of(0, 1, own[1])
    pieces = own_first + own_last[:1]
    pieces += [piece for j in evens for piece in pieces_of(j, 0, even[j][0])]
    total, left_all = add(None, pieces)
    odd[0], total = wait(1, odd[0], total)
    odd[1] = pass_on(1)
    pieces = own_last[1:]
    pieces += [piece for j in odds for piece in pieces_of(j, 0, odd[0][j])]
    pieces += [piece for j in evens for piece in pieces_of(j, 1, even[j][1])]
    total = add(total, pieces)
    odd[1], total = lax.optimization_barrier((odd[1], total))
    pieces = [piece for j in odds for piece in pieces_of(j, 1, odd[1][j])]
    return add(total, pieces, closes=True)


def solution(mesh):
    placed = (
        P("row", "col", None, None, None),
        P("row", "col", None),
        P("row", "col", None, None, None),
        P("row", "col", None),
        P("row", "col", None, None, None),
        P("row", "col", None),
        P("row", None),
    )
    return jax.shard_map(
        per_device, mesh=mesh, in_specs=placed, out_specs=P("row", "col"), check_vma=False
    )
```

```python
import functools

import jax
import jax.numpy as jnp
from jax import lax
from jax.experimental import pallas as pl
from jax.experimental.pallas import tpu as pltpu
from jax.sharding import PartitionSpec as P

CCOLS = 8
PARTS = 2
FIRST_PART = 15, 32
UNROLL = 32
HEAD = 32
HEAD_STEP = 16
VMEM_BYTES = 40 << 20
VMEM = pl.BlockSpec(memory_space=pltpu.VMEM)


def round_up(value, step):
    return value + -value % step


class Sizes:
    def __init__(self, n_stops, n_pairs, n_left, n_right, n_rows, n_col, edge):
        self.n_stops, self.n_pairs, self.n_rows, self.n_col = n_stops, n_pairs, n_rows, n_col
        self.n_left, self.n_right, self.edge = n_left, n_right, edge
        self.parts = PARTS
        first = n_right * FIRST_PART[0] // FIRST_PART[1]
        self.cuts = (0, first, n_right)
        self.per_part = max(first, n_right - first)
        self.zero_slot = n_col * n_left
        self.row_bits = (n_rows - 1).bit_length()
        self.key_bits = self.row_bits + (self.per_part - 1).bit_length()
        self.left_bits = self.zero_slot.bit_length()
        most = (n_pairs + self.per_part * n_rows) // 2
        self.width = round_up(round_up(most, UNROLL) + 1, 128)


def kernel_call(
    kernel,
    out_shape,
    operands,
    scalars=(),
    scratch=(),
    specs=None,
    flops=128,
):
    return pl.pallas_call(
        kernel,
        out_shape=out_shape,
        grid_spec=pltpu.PrefetchScalarGridSpec(
            num_scalar_prefetch=len(scalars),
            in_specs=specs or [VMEM] * len(operands),
            out_specs=jax.tree.map(lambda _: VMEM, out_shape),
            scratch_shapes=list(scratch),
        ),
        compiler_params=pltpu.CompilerParams(vmem_limit_bytes=VMEM_BYTES),
        cost_estimate=pl.CostEstimate(flops=flops, bytes_accessed=128, transcendentals=0),
    )(*scalars, *operands)


def pack_kernel(cuts, blocks_ref, ids_ref, *refs):
    part_refs, head_ref, sems = refs[:-2], refs[-2], refs[-1]
    edge = blocks_ref.shape[1]
    copies = []
    for part, ref in enumerate(part_refs):
        low, count = cuts[part] * edge, (cuts[part + 1] - cuts[part]) * edge
        source, target = blocks_ref.at[pl.ds(low, count)], ref.at[pl.ds(HEAD, count)]
        copies.append(pltpu.make_async_copy(source, target, sems.at[part]))
    for copy in copies:
        copy.start()
    head_ref[...] = jnp.zeros_like(head_ref)
    head_ref[0:1, : ids_ref.shape[1]] = ids_ref[...].astype(jnp.float32)
    for ref in part_refs:
        for row in range(0, HEAD, HEAD_STEP):
            ref[row : row + HEAD_STEP, :] = head_ref[...].astype(ref.dtype)
    for copy in copies:
        copy.wait()


def pack(sizes, blocks, ids):
    edge = sizes.edge
    counts = [high - low for low, high in zip(sizes.cuts, sizes.cuts[1:])]
    shapes = [(HEAD + count * edge, edge) for count in counts]
    return kernel_call(
        functools.partial(pack_kernel, sizes.cuts),
        [jax.ShapeDtypeStruct(shape, blocks.dtype) for shape in shapes],
        [blocks.reshape(-1, edge), ids.reshape(1, -1)],
        scratch=[pltpu.VMEM((HEAD_STEP, edge), jnp.float32), pltpu.SemaphoreType.DMA((PARTS,))],
        specs=[pl.BlockSpec(memory_space=pl.ANY), VMEM],
    )


def ids_of(ref):
    return ref[:HEAD_STEP, :].astype(jnp.float32)[0:1, :]


def prepare_kernel(sizes, count_ref, order_ref, pairs_ref, *refs):
    words_ref = refs[-1]
    id_sets = [ref[...] for ref in refs[:-1]]
    n_col, n_rows, parts = sizes.n_col, sizes.n_rows, sizes.parts
    n_pairs, width = sizes.n_pairs, sizes.width

    def total(mask, value, axis):
        return jnp.sum(jnp.where(mask, value, 0.0), axis=axis, keepdims=True)

    here = lax.axis_index("row")
    lane = lax.broadcasted_iota(jnp.int32, (n_pairs, 128), 1)
    slot = lane[:, : sizes.n_left]
    down = lax.broadcasted_iota(jnp.int32, (n_pairs, 1), 0)
    across = lax.broadcasted_iota(jnp.int32, (1, n_pairs), 1)
    places = lax.broadcasted_iota(jnp.int32, (1, width), 1).astype(jnp.float32)
    dead = float(sizes.n_right * n_rows)
    lefts, keys = [], []
    key_matrix = jnp.zeros((n_pairs, 128), jnp.float32)
    for stop in range(sizes.n_stops):
        ahead = lax.rem(here + stop, n_col)
        ids = id_sets[0]
        for j in range(1, n_col):
            ids = jnp.where(ahead == j, id_sets[j], ids)
        left_row = jnp.zeros(ids.shape, jnp.float32)
        for i in range(n_rows):
            left_row = jnp.where(ids == i, order_ref[:, i : i + 1].astype(jnp.float32), left_row)
        left = pairs_ref[:, 2 * stop : 2 * stop + 1]
        right = pairs_ref[:, 2 * stop + 1 : 2 * stop + 2]
        key = right.astype(jnp.float32) * n_rows + total(slot == left, left_row, 1)
        key = jnp.where(down < count_ref[:, stop : stop + 1], key, dead)
        lefts.append((left + ahead * sizes.n_left - sizes.zero_slot).astype(jnp.float32))
        keys.append(key)
        key_matrix = jnp.where(lane == stop, key, key_matrix)
    key_rows = key_matrix.T
    cut = float(sizes.cuts[1] * n_rows)

    def part_of(key):
        return jnp.where(key >= cut, 1.0, 0.0)

    scale = [float(1 << sizes.key_bits), float(1 << (sizes.key_bits + sizes.left_bits))]
    empty = sizes.zero_slot * (scale[0] + scale[1])
    for stop in range(sizes.n_stops):
        left, key, other = lefts[stop], keys[stop], key_rows[stop : stop + 1, :]
        same = key == other
        rank = total(same & (across < down), 1.0, 1)
        other_rank = total(same & (down < across), 1.0, 0)
        other_opens = other_rank == 2.0 * jnp.floor(other_rank * 0.5)
        own_part, other_part = part_of(key), part_of(other)
        group = jnp.floor(rank * 0.5)
        opens = rank == 2.0 * group
        group += total((other < key) & (own_part == other_part) & other_opens, 1.0, 1)
        word = jnp.where(opens, left * scale[0] + key - own_part * cut, left * scale[1])
        for part in range(parts):
            counted = (own_part == float(part)) & (key < dead)
            words = empty + total(counted & (group == places), word, 0)
            words = jnp.where(places == width - 1.0, total(counted & opens, 1.0, 0), words)
            line = parts * stop + part
            words_ref[line : line + 1, :] = words.astype(jnp.int32)


def products_kernel(sizes, n_rights, layout, opens, closes, words_ref, *refs):
    n_sources = sizes.n_col if opens else 1
    sources, refs = refs[:n_sources], refs[n_sources:]
    right_refs, refs = refs[:n_rights], refs[n_rights:]
    start_ref = None
    if not opens:
        start_ref, refs = refs[0], refs[1:]
    out_ref, refs = refs[0], refs[1:]
    left_ref = sources[0]
    edge = sizes.edge
    if opens:
        left_ref, refs = refs[0], refs[1:]
        rows = sizes.n_left * edge
        for j, source in enumerate(sources):
            left_ref[j * rows : (j + 1) * rows, :] = source[...]
        left_ref[len(sources) * rows :, :] = jnp.zeros((edge, edge), left_ref.dtype)
    ids_ref, col_ref, copy_sem = refs[:3]
    total_ref = refs[3] if closes else out_ref
    for which, ref in enumerate(right_refs):
        ids_ref[which : which + 1, :] = ids_of(ref).astype(jnp.int32)
    copy = pltpu.make_async_copy(ids_ref, col_ref, copy_sem)
    copy.start()
    total_ref[...] = jnp.zeros_like(total_ref) if opens else start_ref[...]
    copy.wait()

    core, col = lax.rem(lax.axis_index("row"), 2), lax.axis_index("col")

    def block(ref, slot, head):
        return ref[pl.ds(pl.multiple_of(slot * edge + head, HEAD_STEP), edge), :]

    for array, head, part, ahead in layout:
        stop = jnp.where(
            core == 0,
            -1 if ahead[0] is None else ahead[0] - col,
            -1 if ahead[1] is None else ahead[1] - col,
        )
        used = (stop >= 0) & (stop < sizes.n_stops)
        line = jnp.clip(stop, 0, sizes.n_stops - 1) * sizes.parts + part
        count = jnp.where(used, words_ref[line, sizes.width - 1], 0)

        def groups(first, size, array=array, head=head, part=part, line=line):
            for member in range(size):
                word = words_ref[line, first + member]
                row = word & ((1 << sizes.row_bits) - 1)
                slot = (word & ((1 << sizes.key_bits) - 1)) >> sizes.row_bits
                word = word >> sizes.key_bits
                lefts = word & ((1 << sizes.left_bits) - 1), word >> sizes.left_bits
                target = row * CCOLS + col_ref[array, slot + sizes.cuts[part]]
                right = block(right_refs[array], slot, head)
                total_ref[target] += jnp.dot(
                    jnp.concatenate([block(left_ref, left, 0) for left in lefts], axis=1),
                    jnp.concatenate([right, right], axis=0),
                    preferred_element_type=jnp.float32,
                )

        steps = (count + UNROLL // 2 - 1) // UNROLL

        @pl.loop(0, steps)
        def _(step, groups=groups):
            groups(step * UNROLL, UNROLL)

        @pl.when(count > steps * UNROLL)
        def _(steps=steps, groups=groups):
            groups(steps * UNROLL, UNROLL // 2)

    if closes:
        for target in range(total_ref.shape[0]):
            row, col = divmod(target, CCOLS)
            out_ref[row * edge : (row + 1) * edge, col * edge : (col + 1) * edge] = total_ref[
                target
            ].astype(out_ref.dtype)


def per_device(a_blocks, a_rows, b_blocks, b_cols, pair_list, pair_count, row_order):
    n_row, n_col = lax.axis_size("row"), lax.axis_size("col")
    n_stops, n_pairs = pair_list.shape[2], pair_list.shape[4]
    sizes = Sizes(
        n_stops,
        n_pairs,
        a_blocks.shape[2],
        b_blocks.shape[2],
        row_order.shape[1],
        n_col,
        a_blocks.shape[3],
    )
    row = lax.axis_index("row")
    edge, sums = sizes.edge, (sizes.n_rows * CCOLS, sizes.edge, sizes.edge)
    reach = n_col + n_stops - 2
    chips = (reach + 1) // 2
    evens, odds = range(2, chips + 1, 2), range(1, chips + 1, 2)
    parts = range(PARTS)

    def from_ahead(block, axis, distance):
        size = lax.axis_size(axis)
        return lax.ppermute(block, axis, [((i + distance) % size, i) for i in range(size)])

    def swap(bit, lower, upper, skip=0):
        mine = lower if lower is upper else jnp.where(row // bit % 2 == 1, upper, lower)
        mine = mine[skip:]
        return lax.ppermute(mine, "row", [(i ^ bit, i) for i in range(n_row)])

    def both(distance):
        return (distance, distance)

    def swapped(j):
        ahead = 2 * j + 1, 2 * j - 1
        return tuple(d if 1 <= d <= reach else None for d in ahead)

    own = pack(sizes, b_blocks, b_cols)
    even = {j: [from_ahead(part, "row", 2 * j) for part in own] for j in range(2, chips + 2, 2)}
    left_ids, left_own = a_rows.reshape(1, -1), a_blocks.reshape(-1, edge)
    left_ids = [left_ids] + [from_ahead(left_ids, "col", j) for j in range(1, n_col)]
    lefts = [left_own] + [from_ahead(left_own, "col", j) for j in range(1, n_col)]
    words = kernel_call(
        functools.partial(prepare_kernel, sizes),
        jax.ShapeDtypeStruct((PARTS * n_stops, sizes.width), jnp.int32),
        [pair_count.reshape(1, -1), row_order, pair_list.reshape(2 * n_stops, n_pairs).T]
        + left_ids,
        flops=1 << 34,
    )

    def wait(part, *others):
        arrived, others = lax.optimization_barrier(([even[j][part] for j in even], others))
        for j, block in zip(even, arrived):
            even[j][part] = block
        return others

    def pass_on(part):
        sets = {0: own, **even}
        return {j: swap(2, sets[j + 1][part], sets[j - 1][part]) for j in odds}

    def add(total, pieces, closes=False):
        rights = list({id(piece[0]): piece[0] for piece in pieces}.values())
        places = {id(block): place for place, block in enumerate(rights)}
        layout = tuple((places[id(piece[0])], *piece[1:]) for piece in pieces)
        if closes:
            out_shape = jax.ShapeDtypeStruct((sizes.n_rows * edge, CCOLS * edge), jnp.bfloat16)
        else:
            out_shape = jax.ShapeDtypeStruct(sums, jnp.float32)
        if total is None:
            left_shape = ((sizes.zero_slot + 1) * edge, edge)
            out_shape = [out_shape, jax.ShapeDtypeStruct(left_shape, b_blocks.dtype)]
        lines = round_up(len(rights), 8)
        return kernel_call(
            functools.partial(
                products_kernel, sizes, len(rights), layout, total is None, closes
            ),
            out_shape,
            (lefts if total is None else [left_all])
            + rights
            + ([] if total is None else [total]),
            [words],
            [
                pltpu.VMEM((lines, 128), jnp.int32),
                pltpu.SMEM((lines, 128), jnp.int32),
                pltpu.SemaphoreType.DMA,
            ]
            + ([pltpu.VMEM(sums, jnp.float32)] if closes else []),
        )

    def pieces_of(j, part, block):
        skip = HEAD_STEP if j in evens else 0
        theirs = swap(1, block, block, skip)
        return [
            (block, HEAD, part, both(2 * j)),
            (theirs, HEAD - skip, part, swapped(j)),
        ]

    odd = {}
    (words,) = wait(0, words)
    odd[0] = pass_on(0)
    own_first, own_last = pieces_of(0, 0, own[0]), pieces_of(0, 1, own[1])
    pieces = own_first + own_last[:1]
    pieces += [piece for j in evens for piece in pieces_of(j, 0, even[j][0])]
    total, left_all = add(None, pieces)
    (total,) = wait(1, total)
    odd[1] = pass_on(1)
    pieces = own_last[1:]
    pieces += [piece for j in odds for piece in pieces_of(j, 0, odd[0][j])]
    pieces += [piece for j in evens for piece in pieces_of(j, 1, even[j][1])]
    total = add(total, pieces)
    odd[1], total = lax.optimization_barrier((odd[1], total))
    pieces = [piece for j in odds for piece in pieces_of(j, 1, odd[1][j])]
    return add(total, pieces, closes=True)


def solution(mesh):
    placed = (
        P("row", "col", None, None, None),
        P("row", "col", None),
        P("row", "col", None, None, None),
        P("row", "col", None),
        P("row", "col", None, None, None),
        P("row", "col", None),
        P("row", None),
    )
    return jax.shard_map(
        per_device, mesh=mesh, in_specs=placed, out_specs=P("row", "col"), check_vma=False
    )
```
